256 devices in a mesh: tm: 16 (over x_lo, z), expert: 16 (over y, x_hi, core).
Axes of the slice: x: 4 (x_hi: 2, x_lo: 2; x = x_hi * 2 + x_lo), y: 4, z: 8, core: 2. Of those that a mesh axis runs over, the one named last changes fastest.
Arguments:
- frames: float32 [32768, 1536], P(('tm', 'expert')), may hold values from -6 to 6
- lengths: int32 [2], replicated, may hold values from 1 to 24576, 32768 in all
- expert_ids: int32 [32768, 2], P(('tm', 'expert')), may hold values from 0 to 15, all different within a row; in each aligned block of 128 rows (0 to 127, 128 to 255, ...) at most 32 rows name the same one
- w_conv: float32 [31, 1536], replicated, may hold values from -1 to 1
- g_norm: float32 [1536], replicated, may hold values from 0.1 to 1.9
- w_router: float32 [1536, 16], replicated, may hold values from -0.15625 to 0.15625
- w_up: bfloat16 [16, 1536, 1536], P('expert'), may hold values from -0.15625 to 0.15625
- w_down: bfloat16 [16, 1536, 1536], P('expert'), may hold values from -0.15625 to 0.15625
- cotangent: float32 [32768, 1536], P(('tm', 'expert')), may hold values from -6 to 6
Outputs:
- block_out: float32 [32768, 1536], P(('tm', 'expert'))
- frames_grad: float32 [32768, 1536], P(('tm', 'expert'))
- conv_grad: float32 [31, 1536], replicated
- gain_grad: float32 [1536], replicated
- router_grad: float32 [1536, 16], replicated
The draws below stay inside these ranges and needn't reach their ends.
Inputs may be any that keep to these rules, and one draw needn't show every extreme that they name: `expert_ids`: within the frames of one device (aligned blocks of 128 frames) no expert is named more than 32 times, a bound that some block reaches. The two experts of a frame differ. The lengths sum to 32768; the longest is at most 24576.
All inputs are finite; a program needn't handle non-finite values.
Results may differ from the reference program's by a relative error of at most 0.02.
Values may be sent and summed in bfloat16 or wider, within the bound.
A program may use at most 128 MiB of HBM per device.

```python
import math
import jax
import jax.numpy as jnp
import numpy as np
from jax import lax

D = 1536
FF = 1536
KS = 31
RECS = 2
F_DEV = 128
EXPERTS = 16
FRAMES = 32768
CAP = 32


def shard_levels(stream_key, dims, cuts, low, largest):
    level = 1.0
    for dim, shards_of in cuts:
        draws = jax.random.uniform(jax.random.fold_in(jax.random.fold_in(stream_key, 6), dim), (shards_of,), jnp.float32, low / len(cuts), largest / len(cuts))
        level = level * jnp.repeat(jnp.exp(draws), dims[dim] // shards_of).reshape((-1,) + (1,) * (len(dims) - 1 - dim))
    return level


def profile(number_of, total, most, lean):
    weights = [(1 << 20) // math.isqrt(rank ** lean) + 1 for rank in range(2, number_of + 1)]
    rest, given = total - most - (number_of - 1), [1] * (number_of - 1)
    while rest > 0:
        free = [i for i in range(number_of - 1) if given[i] < most]
        mass, budget = sum([weights[i] for i in free]), rest
        for i in free:
            addition = min(most - given[i], max(1, budget * weights[i] // mass), rest)
            given[i] = given[i] + addition
            rest = rest - addition
    return np.array([most] + given)


def uneven_parts(own_key, count, total, bound, lean):
    if count == 2:
        one = jax.random.randint(own_key, (), max(1, total - bound), min(bound, total - 1) + 1)
        return jnp.stack([one, total - one])
    sizes = jnp.asarray(profile(count, total, bound, lean), jnp.int32)
    couples = (count - 1) // 2
    donor, sink = sizes[1:1 + 2 * couples:2], sizes[2:2 + 2 * couples:2]
    margin = jnp.minimum(donor - 1, bound - sink)
    moved = jax.random.randint(jax.random.fold_in(own_key, 1), (couples,), 0, 1 << 20) % (margin + 1)
    sizes = sizes.at[1:1 + 2 * couples:2].set(donor - moved).at[2:2 + 2 * couples:2].set(sink + moved)
    return sizes[jax.random.permutation(jax.random.fold_in(own_key, 2), count)]


def deal_out(rng, own, number, rows, amount, top, most, skew):
    order = jax.random.permutation(rng, amount)
    crowded, common = shares(amount, rows * top, most, skew, True), shares(amount, rows * top, most, skew, False)
    places = jnp.arange(amount)

    def named(sizes, turn):
        used = int((sizes > 0).sum())
        fixed = max(1, used // 4)
        moved = fixed + (places - fixed + turn * (used - fixed)) % max(1, amount - fixed)
        return jnp.zeros((amount,), jnp.int32).at[order[jnp.where(places < fixed, places, moved)]].set(jnp.asarray(sizes, jnp.int32))

    sizes = jnp.where(number % 4 == 0, named(crowded, number // 4), named(common, number - number // 4 - 1))
    mixed = jax.random.permutation(jax.random.fold_in(own, 3), amount)
    source_of, taker = mixed[0:amount // 2 * 2:2], mixed[1:amount // 2 * 2:2]
    slack = jnp.minimum(sizes[source_of] - 1, most - sizes[taker]) // 2
    slack = jnp.where((source_of == order[0]) | (taker == order[0]) | (sizes[taker] == 0), 0, jnp.maximum(slack, 0))
    moved = jax.random.randint(jax.random.fold_in(own, 4), (amount // 2,), 0, 1 << 20) % (slack + 1)
    sizes = sizes.at[source_of].add(-moved).at[taker].add(moved)
    items = jnp.searchsorted(jnp.cumsum(sizes), jnp.arange(rows * top), side="right").astype(jnp.int32)
    listing = items.reshape(top, rows).T
    listing = listing[jax.random.permutation(jax.random.fold_in(own, 1), rows)]
    turn = jax.random.randint(jax.random.fold_in(own, 2), (rows, 1), 0, top)
    return jnp.take_along_axis(listing, (jnp.arange(top)[None, :] + turn) % top, axis=1)


def shares(amount, total, most, skew, full):
    portions = [(1 << 20) // math.isqrt(grade ** skew) + 1 for grade in range(1, amount + 1)]
    largest = most if full else min(most, max(-(-total // amount), total * portions[0] // sum(portions)))
    least = 1 if total - largest >= amount - 1 else 0
    holding, spare = [largest] + [least] * (amount - 1), total - largest - least * (amount - 1)
    while spare > 0:
        free = [i for i in range(1, amount) if holding[i] < largest] or [i for i in range(1, amount) if holding[i] < most]
        whole, remaining = sum([portions[i] for i in free]), spare
        for i in free:
            more = min(most - holding[i], max(1, remaining * portions[i] // whole), spare)
            holding[i] = holding[i] + more
            spare = spare - more
    return np.array(holding)


def gaussian(key, dims, width, bound, cuts=(), kind=jnp.bfloat16):
    level = shard_levels(key, dims, cuts, -0.22, 0.18) if cuts else 1.0
    array = jax.random.normal(key, dims, jnp.float32) * width * level
    return jnp.minimum(jnp.maximum(array, -bound), bound).astype(kind)


def setup_inputs(seed: int = 0) -> dict:
    key_of = jax.random.split(jax.random.key(seed), 10)
    frames = gaussian(key_of[0], (FRAMES, D), 1.0, 6.0, ((0, 256),), jnp.float32)
    lengths = uneven_parts(key_of[1], RECS, FRAMES, FRAMES * 3 // 4, 0).astype(jnp.int32)
    expert_ids_keys = jax.random.split(jax.random.fold_in(key_of[2], 1), FRAMES // F_DEV)
    expert_ids_turns = jax.random.permutation(jax.random.fold_in(key_of[2], 3), FRAMES // F_DEV)
    expert_ids = jax.vmap(lambda own, number: deal_out(jax.random.fold_in(key_of[2], 2), own, number, F_DEV, EXPERTS, 2, CAP, 2))(expert_ids_keys, expert_ids_turns).reshape((FRAMES, 2))
    w_conv = gaussian(key_of[3], (KS, D), KS ** -0.5, 1.0, (), jnp.float32)
    g_norm = jnp.clip(1.0 + 0.18 * jax.random.normal(key_of[4], (D,), jnp.float32), 0.1, 1.9)
    w_router = gaussian(key_of[5], (D, EXPERTS), D ** -0.5, 0.15625, (), jnp.float32)
    w_up = gaussian(key_of[6], (EXPERTS, D, FF), D ** -0.5, 0.15625, ((0, 16),))
    w_down = gaussian(key_of[7], (EXPERTS, FF, D), FF ** -0.5, 0.15625, ((0, 16),))
    cotangent = gaussian(key_of[8], (FRAMES, D), 1.0, 6.0, ((0, 256),), jnp.float32)
    return dict(frames=frames, lengths=lengths, expert_ids=expert_ids, w_conv=w_conv, g_norm=g_norm, w_router=w_router, w_up=w_up, w_down=w_down, cotangent=cotangent)


EPS = 1e-06

def recording_of(position, lengths):
    bounds = jnp.cumsum(lengths)[:-1]
    return lax.optimization_barrier(jnp.sum((position[:, None] >= bounds[None, :]).astype(jnp.int32), axis=1))

def conv_terms(widened, labels, w_conv, frame_count):
    kernel_len = w_conv.shape[0]
    half_width = (kernel_len - 1) // 2
    middle = labels[half_width:half_width + frame_count]
    summed = jnp.zeros((frame_count, widened.shape[1]), jnp.float32)
    for offset in range(kernel_len):
        matching = (labels[offset:offset + frame_count] == middle).astype(jnp.float32)
        summed = summed + w_conv[offset][None, :] * widened[offset:offset + frame_count] * matching[:, None]
    return summed

def norm_rows(mixed, g_norm):
    inv_scale = lax.rsqrt(lax.optimization_barrier(jnp.mean(mixed * mixed, axis=-1, keepdims=True)) + EPS)
    return (mixed * inv_scale * g_norm[None, :]).astype(jnp.bfloat16)

def mix_rows(mixed, normed, picked, w_router, expert_ids):
    logits = jnp.dot(normed, w_router, precision=lax.Precision.HIGHEST)
    expert_count = w_router.shape[1]
    chosen = (expert_ids[:, :, None] == jnp.arange(expert_count, dtype=jnp.int32)[None, None, :]).astype(jnp.float32)
    top_logits = jnp.einsum('fke,fe->fk', chosen, logits, precision=lax.Precision.HIGHEST)
    gate_weights = jax.nn.softmax(top_logits, axis=-1)
    return mixed + lax.optimization_barrier(jnp.sum(gate_weights[:, :, None] * picked.astype(jnp.float32), axis=1))

def slot_positions(route_rows, expert_count, capacity):
    flat_ids = route_rows.reshape(-1)
    matches = (flat_ids[:, None] == jnp.arange(expert_count, dtype=jnp.int32)[None, :]).astype(jnp.int32)
    before = jnp.cumsum(matches, axis=0) - matches
    slot_index = lax.optimization_barrier(jnp.sum(before * matches, axis=1))
    return (flat_ids * capacity + slot_index).astype(jnp.int32)

def one_expert(pieces):
    rows_in, up_weight, down_weight = pieces
    hidden = jax.nn.silu(jnp.einsum('scd,df->scf', rows_in.astype(jnp.float32), up_weight.astype(jnp.float32))).astype(jnp.bfloat16)
    return jnp.einsum('scf,fd->scd', hidden.astype(jnp.float32), down_weight.astype(jnp.float32)).astype(jnp.bfloat16)

def forward(frames, w_conv, g_norm, w_router, lengths, expert_ids, w_up, w_down):
    kernel_len = w_conv.shape[0]
    half_width = (kernel_len - 1) // 2
    frame_total = frames.shape[0]
    widened = jnp.pad(frames, ((half_width, half_width), (0, 0)))
    labels = recording_of(jnp.arange(frame_total + 2 * half_width, dtype=jnp.int32) - half_width, lengths)
    pre_act = conv_terms(widened, labels, w_conv, frame_total)
    mixed = frames + jax.nn.silu(pre_act)
    normed = norm_rows(mixed, g_norm).astype(jnp.float32)
    block_count = frame_total // F_DEV
    routes = expert_ids.reshape(block_count, F_DEV, 2)
    positions = jax.vmap(lambda route_rows: slot_positions(route_rows, EXPERTS, CAP))(routes)
    assigned = jnp.broadcast_to(normed.reshape(block_count, F_DEV, 1, D), (block_count, F_DEV, 2, D))
    assigned = assigned.reshape(block_count, 2 * F_DEV, D).astype(jnp.bfloat16)
    buffers = jax.vmap(lambda where_to, values: jnp.zeros((EXPERTS * CAP, D), jnp.bfloat16).at[where_to].set(values))(positions, assigned)
    by_expert = jnp.moveaxis(buffers.reshape(block_count, EXPERTS, CAP, D), 1, 0)
    outputs = lax.map(one_expert, (by_expert, w_up, w_down))
    returned = jnp.moveaxis(outputs, 0, 1).reshape(block_count, EXPERTS * CAP, D)
    picked = jax.vmap(lambda values, where_to: values[where_to])(returned, positions).reshape(frame_total, 2, D)
    return mix_rows(mixed, normed, picked, w_router, expert_ids)

def reference(frames, lengths, expert_ids, w_conv, g_norm, w_router, w_up, w_down, cotangent):

    def local_pass(frames_in, kernel_in, gain_in, router_in):
        return forward(frames_in, kernel_in, gain_in, router_in, lengths, expert_ids, w_up, w_down)
    block_out, pullback = jax.vjp(local_pass, frames, w_conv, g_norm, w_router)
    frames_grad, conv_grad, gain_grad, router_grad = pullback(cotangent)
    return (block_out, frames_grad, conv_grad, gain_grad, router_grad)
```

```python
import jax
import jax.numpy as jnp
from jax import lax
from jax.experimental import pallas as pl
from jax.experimental.pallas import tpu as pltpu
from jax.sharding import PartitionSpec as P

EPS = 1e-06
MESH = pl.DeviceIdType.MESH
F32, BF16 = jnp.float32, jnp.bfloat16
EXACT = lax.Precision.HIGHEST

ROWS = 128
D = 1536
TAPS = 31
EDGE = 16
WIDE = ROWS + 2 * EDGE
SPREAD = WIDE + EDGE
MID = ROWS + EDGE
EXPERTS = 16
CAP = 32
SLOTS = EXPERTS * CAP
LANES = 128
BLOCKS = D // LANES
TILE = 256
TILES = D // TILE
GRADS = 48

NT = (((1,), (1,)), ((), ()))


def sigmoid(v):
    return 0.5 * jnp.tanh(0.5 * v) + 0.5


def spread(wide, bound):
    zeros = jnp.zeros((EDGE, LANES), F32)
    before = jnp.concatenate([wide, zeros], axis=0)
    after = jnp.concatenate([zeros, wide], axis=0)
    row = lax.broadcasted_iota(jnp.int32, (SPREAD, LANES), 0)
    return jnp.where(row < bound, before, jnp.where(row >= bound + EDGE, after, 0.0))


def gather_back(mid, bound):
    row = lax.broadcasted_iota(jnp.int32, (ROWS, LANES), 0) + EDGE
    return jnp.where(row < bound, mid[:ROWS], mid[EDGE:])


def correlate(ref, block, weight_row):
    total = None
    for shift in range(8):
        rows = ref[block, shift : shift + MID + 24, :]
        for whole in range(4):
            tap = 8 * whole + shift - 1
            if 0 <= tap < TAPS:
                term = weight_row(tap) * rows[8 * whole : 8 * whole + MID]
                total = term if total is None else total + term
    return total


def body(
    len_ref, ids_ref, wconv_ref, gain_ref, wr_ref, frames_hbm, cot_hbm, wup_hbm, wdn_hbm,
    out_hbm, dfr_hbm, grad_ref,
    fr, cot, wup, wdn, gw, gd, pre, mixed, dmix, outv, dfrv, normed, cotb,
    onehot, pick, send_c, recv_c, send_x, recv_x, ret_y, got_y, ret_d, got_d,
    dhid, hid, dup, py, pd, parts,
    halo_s, halo_r, ar_src, ar_in, mid_src, mid_in, fin_src, fin,
    lsem, ssem, rsem, hs, hr, a1s, a1r, a2s, a2r, a3s, a3r,
):
    tm, ex = lax.axis_index("tm"), lax.axis_index("expert")
    xl, z = tm // 8, tm % 8
    y, xh, core = ex // 4, (ex // 2) % 2, ex % 2
    lin = tm * EXPERTS + ex

    def peer(r):
        dy, fx, dc = r // 4, (r // 2) % 2, r % 2
        return {
            "tm": ((xl + fx) % 2) * 8 + z,
            "expert": ((y + dy) % 4) * 4 + ((xh + fx) % 2) * 2 + (core + dc) % 2,
        }

    def back(r):
        return ((4 - r // 4) % 4) * 4 + r % 4

    def of_expert(e):
        return ((e // 4 + 4 - y) % 4) * 4 + ((e // 2 + xh) % 2) * 2 + (e + core) % 2

    def column(k):
        return {"tm": (tm + k) % 16, "expert": ex}

    def beside(step):
        other = (lin + 256 + step) % 256
        return {"tm": other // EXPERTS, "expert": other % EXPERTS}

    loads = [
        pltpu.make_async_copy(frames_hbm, fr, lsem.at[0]),
        pltpu.make_async_copy(cot_hbm, cot, lsem.at[1]),
        pltpu.make_async_copy(wdn_hbm.at[0], wdn, lsem.at[2]),
        pltpu.make_async_copy(wup_hbm.at[0], wup, lsem.at[3]),
    ]
    for load in loads:
        load.start()

    barrier = pltpu.get_barrier_semaphore()

    def greet(k, carry):
        pl.semaphore_signal(barrier, inc=1, device_id=peer(k), device_id_type=MESH)
        pl.semaphore_signal(barrier, inc=1, device_id=column(k), device_id_type=MESH)
        return carry

    lax.fori_loop(1, 16, greet, 0)
    pl.semaphore_signal(barrier, inc=1, device_id=beside(1), device_id_type=MESH)
    pl.semaphore_signal(barrier, inc=1, device_id=beside(-1), device_id_type=MESH)

    def upright(row):
        return jnp.broadcast_to(row.astype(F32), (LANES, ROWS)).T.astype(jnp.int32)

    ids0, ids1 = upright(ids_ref[0:1, :]), upright(ids_ref[1:2, :])

    def relative(e):
        return (
            ((((e >> 2) - y) & 3) << 2) | ((((e >> 1) & 1) ^ xh) << 1) | ((e & 1) ^ core)
        )

    rel0, rel1 = relative(ids0), relative(ids1)
    lane = lax.broadcasted_iota(jnp.int32, (ROWS, LANES), 1)
    sub = lax.broadcasted_iota(jnp.int32, (ROWS, LANES), 0)
    names0 = jnp.where(rel0 == lane, 1.0, 0.0).astype(F32)
    names1 = jnp.where(rel1 == lane, 1.0, 0.0).astype(F32)
    names = names0 + names1
    earlier = jnp.where(lane < sub, 1.0, 0.0).astype(F32)
    later = jnp.where(sub < lane, 1.0, 0.0).astype(F32)
    rank = jnp.dot(earlier.astype(BF16), names.astype(BF16), preferred_element_type=F32)
    rank0 = jnp.sum(names0 * rank, axis=1, keepdims=True).astype(jnp.int32)
    rank1 = jnp.sum(names1 * rank, axis=1, keepdims=True).astype(jnp.int32)
    slot0, slot1 = rel0 * CAP + rank0, rel1 * CAP + rank1
    for b in range(4):
        here = slice(b * LANES, (b + 1) * LANES)
        pick[0:ROWS, here] = jnp.where(lane + b * LANES == slot0, 1.0, 0.0).astype(BF16)
        pick[ROWS : 2 * ROWS, here] = jnp.where(lane + b * LANES == slot1, 1.0, 0.0).astype(BF16)
    by_expert = names.T
    order = jnp.dot(by_expert.astype(BF16), later.astype(BF16), preferred_element_type=F32)
    order = jnp.where(by_expert > 0.5, order, -1.0)
    place = lax.broadcasted_iota(jnp.int32, (CAP, LANES), 0).astype(F32)
    for r in range(EXPERTS):
        onehot[r * CAP : (r + 1) * CAP, :] = jnp.where(
            order[r : r + 1, :] == place, 1.0, 0.0
        ).astype(BF16)

    loads[0].wait()
    halo_s[0] = fr[0:EDGE, :].astype(BF16)
    halo_s[1] = fr[ROWS - EDGE : ROWS, :].astype(BF16)

    def halo(stage, side):
        n = 2 * stage + side
        return pltpu.make_async_remote_copy(
            src_ref=halo_s.at[n],
            dst_ref=halo_r.at[2 * stage + 1 - side],
            send_sem=hs.at[n],
            recv_sem=hr.at[2 * stage + 1 - side],
            device_id=beside(2 * side - 1),
            device_id_type=MESH,
        )

    pl.semaphore_wait(barrier, 32)
    halo(0, 0).start()
    halo(0, 1).start()

    def rows_of(ref, r):
        return ref.at[pl.ds(pl.multiple_of(r * CAP, CAP), CAP), :]

    def trade(kind, src, dst, r):
        return pltpu.make_async_remote_copy(
            src_ref=rows_of(src, r),
            dst_ref=rows_of(dst, back(r)),
            send_sem=ssem.at[kind, r],
            recv_sem=rsem.at[kind, back(r)],
            device_id=peer(r),
            device_id_type=MESH,
        )

    def start_batch(kind, src, dst, b):
        def one(i, carry):
            r = 4 * b + i

            @pl.when(r != 0)
            def _():
                trade(kind, src, dst, r).start()

            return carry

        lax.fori_loop(0, 4, one, 0)

    def arrive_batch(kind, src, dst, b):
        def one(i, carry):
            r = 4 * b + i

            @pl.when(r != 0)
            def _():
                trade(kind, src, dst, back(r)).wait_recv()

            return carry

        lax.fori_loop(0, 4, one, 0)

    def cols(n, width=TILE):
        return pl.ds(pl.multiple_of(n * width, width), width)

    def batch(b):
        return pl.ds(pl.multiple_of(b * ROWS, ROWS), ROWS)

    def dispatch(kind, source, src, dst):
        def one(b, carry):
            def part(n, inner):
                src[batch(b), cols(n)] = jnp.dot(
                    onehot[batch(b), :], source[:, cols(n)], preferred_element_type=F32
                ).astype(BF16)
                return inner

            lax.fori_loop(0, TILES, part, 0)
            start_batch(kind, src, dst, b)
            return carry

        lax.fori_loop(0, 4, one, 0)
        dst[0:CAP, :] = src[0:CAP, :]

    loads[1].wait()

    def narrow(n, carry):
        cotb[:, cols(n)] = cot[:, cols(n)].astype(BF16)
        return carry

    lax.fori_loop(0, TILES, narrow, 0)
    dispatch(0, cotb, send_c, recv_c)

    bound = len_ref[0] - lin * ROWS + EDGE
    bound = jnp.where((bound >= 1) & (bound < WIDE), bound, 4 * SPREAD)
    halo(0, 1).wait_recv()
    halo(0, 0).wait_recv()

    def widen(n, middle, stage, m):
        low = jnp.where(lin == 0, 0.0, halo_r[2 * stage, :, cols(m, LANES)].astype(F32))
        high = jnp.where(lin == 255, 0.0, halo_r[2 * stage + 1, :, cols(m, LANES)].astype(F32))
        return jnp.concatenate([low, middle, high], axis=0)

    def conv(m, squares):
        here = cols(m, LANES)
        gw[m] = spread(widen(0, fr[:, here], 0, m), bound)
        total = correlate(gw, m, lambda tap: wconv_ref[tap : tap + 1, here])
        act = gather_back(total, bound)
        row = fr[:, here] + act * sigmoid(act)
        pre[:, here] = act
        mixed[:, here] = row
        return squares + row * row

    squares = lax.fori_loop(0, BLOCKS, conv, jnp.zeros((ROWS, LANES), F32))
    inv = lax.rsqrt(jnp.sum(squares, axis=1, keepdims=True) * (1.0 / D) + EPS)

    def norm(m, carry):
        here = cols(m, LANES)
        normed[:, here] = (mixed[:, here] * inv * gain_ref[:, here]).astype(BF16)
        return carry

    lax.fori_loop(0, BLOCKS, norm, 0)
    dispatch(1, normed, send_x, recv_x)

    logits = lax.dot_general(
        normed[...].astype(F32), wr_ref[...], NT, precision=EXACT, preferred_element_type=F32
    )
    lane16 = lane[:, 0:EXPERTS]
    ids16 = ids0[:, 0:EXPERTS], ids1[:, 0:EXPERTS]
    top0 = jnp.sum(jnp.where(ids16[0] == lane16, logits, 0.0), axis=1, keepdims=True)
    top1 = jnp.sum(jnp.where(ids16[1] == lane16, logits, 0.0), axis=1, keepdims=True)
    most = jnp.maximum(top0, top1)
    exp0, exp1 = jnp.exp(top0 - most), jnp.exp(top1 - most)
    gate0, gate1 = exp0 / (exp0 + exp1), exp1 / (exp0 + exp1)

    loads[2].wait()

    def hidden_grad(b, carry):
        arrive_batch(0, send_c, recv_c, b)

        def part(n, inner):
            dhid[batch(b), cols(n)] = lax.dot_general(
                recv_c[batch(b), :], wdn[cols(n), :], NT, preferred_element_type=F32
            ).astype(BF16)
            return inner

        lax.fori_loop(0, TILES, part, 0)
        return carry

    lax.fori_loop(0, 4, hidden_grad, 0)
    loads[3].wait()

    def expert(b, carry):
        arrive_batch(1, send_x, recv_x, b)

        def up(n, inner):
            u = jnp.dot(recv_x[batch(b), :], wup[:, cols(n)], preferred_element_type=F32)
            s = sigmoid(u)
            hid[:, cols(n)] = (u * s).astype(BF16)
            slope = s * (1.0 + u * (1.0 - s))
            dup[:, cols(n)] = (dhid[batch(b), cols(n)].astype(F32) * slope).astype(BF16)
            return inner

        def down(n, inner):
            ret_y[batch(b), cols(n)] = jnp.dot(
                hid[...], wdn[:, cols(n)], preferred_element_type=F32
            ).astype(BF16)
            return inner

        def rows_grad(n, inner):
            ret_d[batch(b), cols(n)] = lax.dot_general(
                dup[...], wup[cols(n), :], NT, preferred_element_type=F32
            ).astype(BF16)
            return inner

        lax.fori_loop(0, TILES, up, 0)
        lax.fori_loop(0, TILES, down, 0)
        start_batch(2, ret_y, got_y, b)
        lax.fori_loop(0, TILES, rows_grad, 0)
        start_batch(3, ret_d, got_d, b)
        return carry

    lax.fori_loop(0, 4, expert, 0)
    got_y[0:CAP, :] = ret_y[0:CAP, :]
    got_d[0:CAP, :] = ret_d[0:CAP, :]

    def collect(kind, src, got, total):
        for b in range(4):
            arrive_batch(kind, src, got, b)

            def part(n, carry):
                term = jnp.dot(
                    pick[:, b * ROWS : (b + 1) * ROWS],
                    got[batch(b), cols(n)],
                    preferred_element_type=F32,
                )
                total[:, cols(n)] = term if b == 0 else total[:, cols(n)] + term
                return carry

            lax.fori_loop(0, TILES, part, 0)

    collect(2, ret_y, got_y, py)

    def finish(m, sums):
        here = cols(m, LANES)
        first, second = py[0:ROWS, here], py[ROWS : 2 * ROWS, here]
        outv[:, here] = mixed[:, here] + (gate0 * first + gate1 * second)
        c = cot[:, here]
        return sums + c * (first - second)

    sums = lax.fori_loop(0, BLOCKS, finish, jnp.zeros((ROWS, LANES), F32))
    store_out = pltpu.make_async_copy(outv, out_hbm, lsem.at[4])
    store_out.start()
    dtop = gate0 * gate1 * jnp.sum(sums, axis=1, keepdims=True)
    dlogits = jnp.where(ids0 == lane, dtop, 0.0) - jnp.where(ids1 == lane, dtop, 0.0)
    dlogits_t = dlogits.T[0:EXPERTS, :]
    dlogits = dlogits[:, 0:EXPERTS]

    def router(m, carry):
        here = cols(m, LANES)
        ar_src[m, 32:48, :] = jnp.dot(
            dlogits_t, normed[:, here].astype(F32), precision=EXACT, preferred_element_type=F32
        ).astype(BF16)
        dmix[:, here] = jnp.dot(
            dlogits, wr_ref[:, here], precision=EXACT, preferred_element_type=F32
        )
        return carry

    lax.fori_loop(0, BLOCKS, router, 0)

    collect(3, ret_d, got_d, pd)

    def norm_back(m, sums):
        here = cols(m, LANES)
        dn = gate0 * pd[0:ROWS, here] + gate1 * pd[ROWS : 2 * ROWS, here] + dmix[:, here]
        row = mixed[:, here]
        parts[m, 0:8, :] = jnp.sum((dn * row * inv).reshape(ROWS // 8, 8, LANES), axis=0)
        dn = dn * gain_ref[:, here]
        pd[0:ROWS, here] = dn
        return sums + dn * row

    sums = lax.fori_loop(0, BLOCKS, norm_back, jnp.zeros((ROWS, LANES), F32))
    pull = inv * inv * inv * (jnp.sum(sums, axis=1, keepdims=True) * (1.0 / D))

    def act_back(m, carry):
        here = cols(m, LANES)
        dm = cot[:, here] + (inv * pd[0:ROWS, here] - mixed[:, here] * pull)
        act = pre[:, here]
        s = sigmoid(act)
        dp = dm * (s * (1.0 + act * (1.0 - s)))
        dmix[:, here] = dm
        pd[ROWS : 2 * ROWS, here] = dp
        halo_s[2, :, here] = dp[0:EDGE].astype(BF16)
        halo_s[3, :, here] = dp[ROWS - EDGE : ROWS].astype(BF16)
        return carry

    lax.fori_loop(0, BLOCKS, act_back, 0)
    halo(1, 0).start()
    halo(1, 1).start()

    rows32 = lax.broadcasted_iota(jnp.int32, (32, 256), 0)
    lanes32 = lax.broadcasted_iota(jnp.int32, (32, 256), 1)
    fold = jnp.where((lanes32 >> 3) == rows32, 1.0, 0.0).astype(F32)

    def to_owner(m):
        r = of_expert(m)
        return pltpu.make_async_remote_copy(
            src_ref=ar_src.at[m],
            dst_ref=ar_in.at[back(r)],
            send_sem=a1s.at[m],
            recv_sem=a1r.at[back(r)],
            device_id=peer(r),
            device_id_type=MESH,
        )

    def kernel_grad(i, carry):
        m = (i + ex) % BLOCKS
        here = cols(m, LANES)
        edge = jnp.zeros((EDGE, LANES), F32)
        mid = spread(jnp.concatenate([edge, pd[ROWS : 2 * ROWS, here], edge], axis=0), bound)
        mid = mid[EDGE : EDGE + MID]
        terms = [None] * TAPS
        for shift in range(8):
            rows = gw[m, shift : shift + MID + 24, :]
            for whole in range(4):
                tap = 8 * whole + shift - 1
                if 0 <= tap < TAPS:
                    product = mid * rows[8 * whole : 8 * whole + MID]
                    terms[tap] = jnp.sum(product.reshape(MID // 8, 8, LANES), axis=0)
        terms.append(parts[m, 0:8, :])
        ar_src[m, 0:32, :] = jnp.dot(
            fold, jnp.concatenate(terms, axis=0), precision=EXACT, preferred_element_type=F32
        ).astype(BF16)

        @pl.when(m != ex)
        def _():
            to_owner(m).start()

        return carry

    lax.fori_loop(0, BLOCKS, kernel_grad, 0)

    halo(1, 1).wait_recv()
    halo(1, 0).wait_recv()

    def frames_back(m, carry):
        here = cols(m, LANES)
        gd[0] = spread(widen(0, pd[ROWS : 2 * ROWS, here], 1, m), bound)
        total = correlate(gd, 0, lambda tap: wconv_ref[TAPS - 1 - tap : TAPS - tap, here])
        dfrv[:, here] = dmix[:, here] + gather_back(total, bound)
        return carry

    lax.fori_loop(0, BLOCKS // 2, frames_back, 0)

    def over_columns(k):
        return pltpu.make_async_remote_copy(
            src_ref=mid_src,
            dst_ref=mid_in.at[16 - k],
            send_sem=a2s.at[k],
            recv_sem=a2r.at[16 - k],
            device_id=column(k),
            device_id_type=MESH,
        )

    def to_all(r):
        return pltpu.make_async_remote_copy(
            src_ref=fin_src,
            dst_ref=fin.at[ex],
            send_sem=a3s.at[r],
            recv_sem=a3r.at[ex],
            device_id=peer(r),
            device_id_type=MESH,
        )

    @pl.when(ex < BLOCKS)
    def _():
        def add(q, total):
            pltpu.make_async_remote_copy(
                src_ref=ar_src.at[0],
                dst_ref=ar_in.at[q],
                send_sem=a1s.at[0],
                recv_sem=a1r.at[q],
                device_id=peer(q),
                device_id_type=MESH,
            ).wait_recv()
            return total + ar_in[q].astype(F32)

        total = lax.fori_loop(1, 16, add, ar_src[ex].astype(F32))
        mid_src[...] = total.astype(BF16)

        def send(k, carry):
            over_columns(k).start()
            return carry

        lax.fori_loop(1, 16, send, 0)

    lax.fori_loop(BLOCKS // 2, BLOCKS, frames_back, 0)
    store_dfr = pltpu.make_async_copy(dfrv, dfr_hbm, lsem.at[5])
    store_dfr.start()

    @pl.when(ex < BLOCKS)
    def _():
        def add(k, total):
            over_columns(16 - k).wait_recv()
            return total + mid_in[k].astype(F32)

        total = lax.fori_loop(1, 16, add, mid_src[...].astype(F32))
        fin_src[...] = total.astype(BF16)

        def send(r, carry):
            to_all(r).start()
            return carry

        lax.fori_loop(1, 16, send, 0)
        fin[ex] = fin_src[...]

    def spread_out(m, carry):
        @pl.when(m != ex)
        def _():
            pltpu.make_async_remote_copy(
                src_ref=fin_src,
                dst_ref=fin.at[m],
                send_sem=a3s.at[0],
                recv_sem=a3r.at[m],
                device_id=peer(of_expert(m)),
                device_id_type=MESH,
            ).wait_recv()

        grad_ref[:, cols(m, LANES)] = fin[m].astype(F32)
        return carry

    lax.fori_loop(0, BLOCKS, spread_out, 0)

    def sent(r, carry):
        trade(0, send_c, recv_c, r).wait_send()
        trade(1, send_x, recv_x, r).wait_send()
        trade(2, ret_y, got_y, r).wait_send()
        trade(3, ret_d, got_d, r).wait_send()
        return carry

    lax.fori_loop(1, 16, sent, 0)

    def sent_owner(m, carry):
        @pl.when(m != ex)
        def _():
            to_owner(m).wait_send()

        return carry

    lax.fori_loop(0, BLOCKS, sent_owner, 0)

    @pl.when(ex < BLOCKS)
    def _():
        def done(k, carry):
            over_columns(k).wait_send()
            to_all(k).wait_send()
            return carry

        lax.fori_loop(1, 16, done, 0)

    for stage in range(2):
        for side in range(2):
            halo(stage, side).wait_send()
    store_out.wait()
    store_dfr.wait()


def on_device(frames, lengths, expert_ids, w_conv, g_norm, w_router, w_up, w_down, cotangent):
    vmem = pl.BlockSpec(memory_space=pltpu.VMEM)
    smem = pl.BlockSpec(memory_space=pltpu.SMEM)
    anywhere = pl.BlockSpec(memory_space=pl.ANY)
    wide_f = pltpu.VMEM((ROWS, D), F32)
    slots = pltpu.VMEM((SLOTS, D), BF16)
    weight = pltpu.VMEM((D, D), BF16)
    dma = pltpu.SemaphoreType.DMA
    block_out, frames_grad, grads = pl.pallas_call(
        body,
        out_shape=(
            jax.ShapeDtypeStruct((ROWS, D), F32),
            jax.ShapeDtypeStruct((ROWS, D), F32),
            jax.ShapeDtypeStruct((GRADS, D), F32),
        ),
        in_specs=[smem, vmem, vmem, vmem, vmem, anywhere, anywhere, anywhere, anywhere],
        out_specs=(anywhere, anywhere, vmem),
        scratch_shapes=[
            wide_f, wide_f, weight, weight,
            pltpu.VMEM((BLOCKS, SPREAD, LANES), F32),
            pltpu.VMEM((1, SPREAD, LANES), F32),
            wide_f, wide_f, wide_f, wide_f, wide_f,
            pltpu.VMEM((ROWS, D), BF16), pltpu.VMEM((ROWS, D), BF16),
            pltpu.VMEM((SLOTS, ROWS), BF16), pltpu.VMEM((2 * ROWS, SLOTS), BF16),
            slots, slots, slots, slots, slots, slots, slots, slots,
            slots, pltpu.VMEM((ROWS, D), BF16), pltpu.VMEM((ROWS, D), BF16),
            pltpu.VMEM((2 * ROWS, D), F32), pltpu.VMEM((2 * ROWS, D), F32),
            pltpu.VMEM((BLOCKS, 8, LANES), F32),
            pltpu.VMEM((4, EDGE, D), BF16), pltpu.VMEM((4, EDGE, D), BF16),
            pltpu.VMEM((BLOCKS, GRADS, LANES), BF16), pltpu.VMEM((16, GRADS, LANES), BF16),
            pltpu.VMEM((GRADS, LANES), BF16), pltpu.VMEM((16, GRADS, LANES), BF16),
            pltpu.VMEM((GRADS, LANES), BF16), pltpu.VMEM((BLOCKS, GRADS, LANES), BF16),
            dma((6,)), dma((4, 16)), dma((4, 16)), dma((4,)), dma((4,)),
            dma((BLOCKS,)), dma((16,)), dma((16,)), dma((16,)), dma((16,)), dma((BLOCKS,)),
        ],
        compiler_params=pltpu.CompilerParams(
            collective_id=0, has_side_effects=True, vmem_limit_bytes=56 * 2**20
        ),
    )(
        lengths, expert_ids.T, w_conv, g_norm.reshape(1, D), w_router.T,
        frames, cotangent, w_up, w_down,
    )
    return block_out, frames_grad, grads[:TAPS], grads[TAPS], grads[32:].T


def solution(mesh):
    placed = (
        P(("tm", "expert"), None),
        P(),
        P(("tm", "expert"), None),
        P(),
        P(),
        P(),
        P("expert", None, None),
        P("expert", None, None),
        P(("tm", "expert"), None),
    )
    return jax.shard_map(
        on_device,
        mesh=mesh,
        in_specs=placed,
        out_specs=(P(("tm", "expert"), None), P(("tm", "expert"), None), P(), P(), P()),
        check_vma=False,
    )
```

```python
import jax
import jax.numpy as jnp
from jax import lax
from jax.experimental import pallas as pl
from jax.experimental.pallas import tpu as pltpu
from jax.sharding import PartitionSpec as P

EPS = 1e-06
MESH = pl.DeviceIdType.MESH
F32, BF16 = jnp.float32, jnp.bfloat16
EXACT = lax.Precision.HIGHEST

ROWS = 128
D = 1536
TAPS = 31
EDGE = 16
WIDE = ROWS + 2 * EDGE
SPREAD = WIDE + EDGE
MID = ROWS + EDGE
EXPERTS = 16
CAP = 32
SLOTS = EXPERTS * CAP
LANES = 128
BLOCKS = D // LANES
TILE = 256
TILES = D // TILE
GRADS = 48
DE = D + LANES

NT = (((1,), (1,)), ((), ()))


def sigmoid(v):
    return 0.5 * jnp.tanh(0.5 * v) + 0.5


def spread(wide, bound):
    zeros = jnp.zeros((EDGE, LANES), F32)
    before = jnp.concatenate([wide, zeros], axis=0)
    after = jnp.concatenate([zeros, wide], axis=0)
    row = lax.broadcasted_iota(jnp.int32, (SPREAD, LANES), 0)
    return jnp.where(row < bound, before, jnp.where(row >= bound + EDGE, after, 0.0))


def gather_back(mid, bound):
    row = lax.broadcasted_iota(jnp.int32, (ROWS, LANES), 0) + EDGE
    return jnp.where(row < bound, mid[:ROWS], mid[EDGE:])


def correlate(ref, block, weight_row):
    total = None
    for shift in range(8):
        rows = ref[block, shift : shift + MID + 24, :]
        for whole in range(4):
            tap = 8 * whole + shift - 1
            if 0 <= tap < TAPS:
                term = weight_row(tap) * rows[8 * whole : 8 * whole + MID]
                total = term if total is None else total + term
    return total


def body(
    len_hbm, ids_hbm, wconv_hbm, gain_hbm, wr_hbm, frames_hbm, cot_hbm, wup_hbm, wdn_hbm,
    outv, dfrv, convv, gainv, routerv,
    len_ref, ids_ref, wconv_ref, gain_ref, wr_ref, wrb,
    fr, cot, wup, wdn, gw, gd, pre, mixed, dmix,
    normed, cotb,
    onehot, pick, send_c, recv_c, send_x, recv_x, ret_y, got_y, ret_d, got_d,
    dhid, hid, dup, py, pd, pg, parts,
    halo_s, halo_r, ar_src, ar_in, mid_src, mid_in, fin_src, fin,
    lsem, ssem, rsem, hs, hr, a1s, a1r, a2s, a2r, a3s, a3r, known,
):
    tm, ex = lax.axis_index("tm"), lax.axis_index("expert")
    xl, z = tm // 8, tm % 8
    y, xh, core = ex // 4, (ex // 2) % 2, ex % 2
    lin = tm * EXPERTS + ex

    def peer(r):
        b, dy = r // 4, r % 4
        fx, dc = (dy + b // 2) % 2, b % 2
        return {
            "tm": ((xl + fx) % 2) * 8 + z,
            "expert": ((y + dy) % 4) * 4 + ((xh + fx) % 2) * 2 + (core + dc) % 2,
        }

    def back(r):
        return (r // 4) * 4 + (4 - r % 4) % 4

    def of_expert(e):
        dy, fx, dc = (e // 4 + 4 - y) % 4, (e // 2 + xh) % 2, (e + core) % 2
        return 4 * (2 * ((dy + fx) % 2) + dc) + dy

    def column(k):
        return {"tm": (tm + k) % 16, "expert": ex}

    def along(step):
        return {"tm": xl * 8 + (z + 8 + step) % 8, "expert": ex}

    def beside(step):
        other = (lin + 256 + step) % 256
        return {"tm": other // EXPERTS, "expert": other % EXPERTS}

    barrier = pltpu.get_barrier_semaphore()
    hails = [peer(r) for r in (6, 2, 14, 10, 7, 5, 3, 1, 15, 13, 11, 9, 12, 8, 4)]
    hails = hails[:4] + [beside(1), beside(-1)] + hails[4:] + [along(1), along(-1), column(8)]
    loads = [
        pltpu.make_async_copy(frames_hbm, fr, lsem.at[0]),
        pltpu.make_async_copy(cot_hbm, cot, lsem.at[1]),
        pltpu.make_async_copy(wdn_hbm.at[0], wdn, lsem.at[2]),
        pltpu.make_async_copy(wup_hbm.at[0], wup, lsem.at[3]),
        pltpu.make_async_copy(ids_hbm, ids_ref, lsem.at[4]),
        pltpu.make_async_copy(wconv_hbm, wconv_ref, lsem.at[5]),
        pltpu.make_async_copy(gain_hbm, gain_ref, lsem.at[6]),
        pltpu.make_async_copy(wr_hbm, wr_ref, lsem.at[7]),
        pltpu.make_async_copy(len_hbm, len_ref, lsem.at[8]),
    ]
    for n in (4, 0, 1):
        loads[n].start()
    for other in hails:
        pl.semaphore_signal(barrier, inc=1, device_id=other, device_id_type=MESH)
    for n in (8, 5, 6, 7, 2, 3):
        loads[n].start()

    loads[4].wait()
    def upright(row):
        return jnp.broadcast_to(row.astype(F32), (LANES, ROWS)).T.astype(jnp.int32)

    ids0, ids1 = upright(ids_ref[0:1, :]), upright(ids_ref[1:2, :])

    def relative(e):
        dy, fx, dc = ((e >> 2) - y) & 3, ((e >> 1) & 1) ^ xh, (e & 1) ^ core
        return (((dy ^ fx) & 1) << 3) | (dc << 2) | dy

    rel0, rel1 = relative(ids0), relative(ids1)
    lane = lax.broadcasted_iota(jnp.int32, (ROWS, LANES), 1)
    sub = lax.broadcasted_iota(jnp.int32, (ROWS, LANES), 0)
    names0 = jnp.where(rel0 == lane, 1.0, 0.0).astype(F32)
    names1 = jnp.where(rel1 == lane, 1.0, 0.0).astype(F32)
    names = names0 + names1
    earlier = jnp.where(lane < sub, 1.0, 0.0).astype(F32)
    later = jnp.where(sub < lane, 1.0, 0.0).astype(F32)
    rank = jnp.dot(earlier.astype(BF16), names.astype(BF16), preferred_element_type=F32)
    rank0 = jnp.sum(names0 * rank, axis=1, keepdims=True).astype(jnp.int32)
    rank1 = jnp.sum(names1 * rank, axis=1, keepdims=True).astype(jnp.int32)
    slot0, slot1 = rel0 * CAP + rank0, rel1 * CAP + rank1
    for b in range(4):
        here = slice(b * LANES, (b + 1) * LANES)
        pick[0:ROWS, here] = jnp.where(lane + b * LANES == slot0, 1.0, 0.0).astype(BF16)
        pick[ROWS : 2 * ROWS, here] = jnp.where(lane + b * LANES == slot1, 1.0, 0.0).astype(BF16)
    by_expert = names.T
    order = jnp.dot(by_expert.astype(BF16), later.astype(BF16), preferred_element_type=F32)
    order = jnp.where(by_expert > 0.5, order, -1.0)
    place = lax.broadcasted_iota(jnp.int32, (CAP, LANES), 0).astype(F32)
    for r in range(EXPERTS):
        onehot[r * CAP : (r + 1) * CAP, :] = jnp.where(
            order[r : r + 1, :] == place, 1.0, 0.0
        ).astype(BF16)

    loads[0].wait()
    halo_s[0] = fr[0:EDGE, :].astype(BF16)
    halo_s[1] = fr[ROWS - EDGE : ROWS, :].astype(BF16)

    def halo(stage, side):
        n = 2 * stage + side
        return pltpu.make_async_remote_copy(
            src_ref=halo_s.at[n],
            dst_ref=halo_r.at[2 * stage + 1 - side],
            send_sem=hs.at[n],
            recv_sem=hr.at[2 * stage + 1 - side],
            device_id=beside(2 * side - 1),
            device_id_type=MESH,
        )

    def rows_of(ref, r):
        return ref.at[pl.ds(pl.multiple_of(r * CAP, CAP), CAP), :]

    def trade(kind, src, dst, r):
        return pltpu.make_async_remote_copy(
            src_ref=rows_of(src, r),
            dst_ref=rows_of(dst, back(r)),
            send_sem=ssem.at[kind, r],
            recv_sem=rsem.at[kind, back(r)],
            device_id=peer(r),
            device_id_type=MESH,
        )

    def start_batch(kind, src, dst, b):
        def one(i, carry):
            r = 4 * b + i

            @pl.when(r != 0)
            def _():
                trade(kind, src, dst, r).start()

            return carry

        lax.fori_loop(0, 4, one, 0)

    def arrive_batch(kind, src, dst, b):
        def one(i, carry):
            r = 4 * b + i

            @pl.when(r != 0)
            def _():
                trade(kind, src, dst, back(r)).wait_recv()

            return carry

        lax.fori_loop(0, 4, one, 0)

    def cols(n, width=TILE):
        return pl.ds(pl.multiple_of(n * width, width), width)

    def batch(b):
        return pl.ds(pl.multiple_of(b * ROWS, ROWS), ROWS)

    def fill(source, src, b):
        def part(n, inner):
            src[batch(b), cols(n)] = jnp.dot(
                onehot[batch(b), :], source[:, cols(n)], preferred_element_type=F32
            ).astype(BF16)
            return inner

        lax.fori_loop(0, TILES, part, 0)

    loads[1].wait()

    def narrow(n, carry):
        cotb[:, cols(n)] = cot[:, cols(n)].astype(BF16)
        return carry

    lax.fori_loop(0, TILES, narrow, 0)

    def fill_c(b, carry):
        fill(cotb, send_c, b)
        return carry

    lax.fori_loop(0, 4, fill_c, 0)
    pl.semaphore_wait(barrier, len(hails))
    halo(0, 0).start()
    halo(0, 1).start()

    def go_c(b, carry):
        start_batch(0, send_c, recv_c, b)
        return carry

    lax.fori_loop(0, 4, go_c, 0)
    recv_c[0:CAP, :] = send_c[0:CAP, :]

    def tell(n):
        pl.semaphore_signal(known.at[2 * n], inc=1, device_id=along(1), device_id_type=MESH)
        pl.semaphore_signal(known.at[2 * n + 1], inc=1, device_id=along(-1), device_id_type=MESH)

    def hear(n):
        pl.semaphore_wait(known.at[2 * n], 1)
        pl.semaphore_wait(known.at[2 * n + 1], 1)

    tell(0)

    loads[8].wait()
    loads[5].wait()
    bound = len_ref[0] - lin * ROWS + EDGE
    bound = jnp.where((bound >= 1) & (bound < WIDE), bound, 4 * SPREAD)
    halo(0, 1).wait_recv()
    halo(0, 0).wait_recv()

    def widen(n, middle, stage, m):
        low = jnp.where(lin == 0, 0.0, halo_r[2 * stage, :, cols(m, LANES)].astype(F32))
        high = jnp.where(lin == 255, 0.0, halo_r[2 * stage + 1, :, cols(m, LANES)].astype(F32))
        return jnp.concatenate([low, middle, high], axis=0)

    def conv(m, squares):
        here = cols(m, LANES)
        gw[m] = spread(widen(0, fr[:, here], 0, m), bound)
        total = correlate(gw, m, lambda tap: wconv_ref[tap : tap + 1, here])
        act = gather_back(total, bound)
        row = fr[:, here] + act * sigmoid(act)
        pre[:, here] = act
        mixed[:, here] = row
        return squares + row * row

    squares = lax.fori_loop(0, BLOCKS, conv, jnp.zeros((ROWS, LANES), F32))
    inv = lax.rsqrt(jnp.sum(squares, axis=1, keepdims=True) * (1.0 / D) + EPS)

    loads[6].wait()

    def gain(here):
        return gain_ref[here].reshape(1, LANES)

    def norm(m, carry):
        here = cols(m, LANES)
        normed[:, here] = (mixed[:, here] * inv * gain(here)).astype(BF16)
        return carry

    lax.fori_loop(0, BLOCKS, norm, 0)

    def go_x(b, carry):
        fill(normed, send_x, b)
        start_batch(1, send_x, recv_x, b)
        return carry

    lax.fori_loop(0, 4, go_x, 0)
    recv_x[0:CAP, :] = send_x[0:CAP, :]
    hear(0)
    tell(1)

    loads[7].wait()
    router_f = wr_ref[...]
    part0 = router_f.astype(BF16)
    rest = router_f - part0.astype(F32)
    part1 = rest.astype(BF16)
    wrb[0:16, :] = part0
    wrb[16:32, :] = part1
    wrb[32:48, :] = (rest - part1.astype(F32)).astype(BF16)
    wrb[48:64, :] = part0
    wrb[64:128, :] = jnp.zeros((64, D), BF16)
    logits = lax.dot_general(normed[...], wrb[...], NT, preferred_element_type=F32)
    logits = jnp.where(lane < 48, logits, 0.0)
    low = lane & 15
    top0 = jnp.sum(jnp.where(ids0 == low, logits, 0.0), axis=1, keepdims=True)
    top1 = jnp.sum(jnp.where(ids1 == low, logits, 0.0), axis=1, keepdims=True)
    most = jnp.maximum(top0, top1)
    exp0, exp1 = jnp.exp(top0 - most), jnp.exp(top1 - most)
    gate0, gate1 = exp0 / (exp0 + exp1), exp1 / (exp0 + exp1)

    loads[2].wait()

    def hidden_grad(b, carry):
        arrive_batch(0, send_c, recv_c, b)

        def part(n, inner):
            dhid[batch(b), cols(n)] = lax.dot_general(
                recv_c[batch(b), :], wdn[cols(n), :], NT, preferred_element_type=F32
            ).astype(BF16)
            return inner

        lax.fori_loop(0, TILES, part, 0)
        return carry

    lax.fori_loop(0, 4, hidden_grad, 0)
    hear(1)
    tell(2)
    loads[3].wait()

    def expert(b, carry):
        arrive_batch(1, send_x, recv_x, b)

        def up(n, dots):
            u = jnp.dot(recv_x[batch(b), :], wup[:, cols(n)], preferred_element_type=F32)
            s = sigmoid(u)
            h = (u * s).astype(BF16)
            hid[batch(b), cols(n)] = h
            slope = s * (1.0 + u * (1.0 - s))
            dh = dhid[batch(b), cols(n)].astype(F32)
            dup[:, cols(n)] = (dh * slope).astype(BF16)
            dot = dh * h.astype(F32)
            return dots + dot[:, :LANES] + dot[:, LANES:]

        def rows_grad(n, inner):
            ret_d[batch(b), cols(n)] = lax.dot_general(
                dup[...], wup[cols(n), :], NT, preferred_element_type=F32
            ).astype(BF16)
            return inner

        dots = lax.fori_loop(0, TILES, up, jnp.zeros((ROWS, LANES), F32))
        dgate = jnp.sum(dots, axis=1, keepdims=True)
        first = dgate.astype(BF16).astype(F32)
        ret_d[batch(b), D:DE] = jnp.where(
            lane == 0, first, jnp.where(lane == 1, dgate - first, 0.0)
        ).astype(BF16)
        lax.fori_loop(0, TILES, rows_grad, 0)
        start_batch(3, ret_d, got_d, b)
        return carry

    lax.fori_loop(0, 4, expert, 0)
    got_d[0:CAP, :] = ret_d[0:CAP, :]

    def down(b, carry):
        def part(n, inner):
            ret_y[batch(b), cols(n)] = jnp.dot(
                hid[batch(b), :], wdn[:, cols(n)], preferred_element_type=F32
            ).astype(BF16)
            return inner

        lax.fori_loop(0, TILES, part, 0)
        start_batch(2, ret_y, got_y, b)
        return carry

    lax.fori_loop(0, 4, down, 0)
    got_y[0:CAP, :] = ret_y[0:CAP, :]
    hear(2)
    tell(3)

    def collect(kind, src, got, total, tail):
        for b in range(4):
            arrive_batch(kind, src, got, b)
            chosen = pick[:, b * ROWS : (b + 1) * ROWS]

            def part(n, carry):
                term = jnp.dot(chosen, got[batch(b), cols(n)], preferred_element_type=F32)
                total[:, cols(n)] = term if b == 0 else total[:, cols(n)] + term
                return carry

            lax.fori_loop(0, TILES, part, 0)
            if tail is not None:
                term = jnp.dot(chosen, got[batch(b), D:DE], preferred_element_type=F32)
                tail[...] = term if b == 0 else tail[...] + term

    collect(3, ret_d, got_d, pd, pg)
    dgates = jnp.sum(pg[...], axis=1, keepdims=True)
    dtop = gate0 * gate1 * (dgates[0:ROWS] - dgates[ROWS : 2 * ROWS])
    first = dtop.astype(BF16).astype(F32)
    second = dtop - first
    amount = jnp.where(lane < 48, first, jnp.where(lane < 64, second, 0.0))
    dlogits = jnp.where(ids0 == low, amount, 0.0) - jnp.where(ids1 == low, amount, 0.0)
    dlogits_t = dlogits.T[32:64, :].astype(BF16)
    dlogits = dlogits.astype(BF16)

    def router(n, carry):
        both = jnp.dot(dlogits_t, normed[:, cols(n)], preferred_element_type=F32)
        both = (both[0:16] + both[16:32]).astype(BF16)
        ar_src[2 * n, 32:48, :] = both[:, :LANES]
        ar_src[2 * n + 1, 32:48, :] = both[:, LANES:]
        dmix[:, cols(n)] = jnp.dot(dlogits, wrb[:, cols(n)], preferred_element_type=F32)
        return carry

    lax.fori_loop(0, TILES, router, 0)

    def norm_back(m, sums):
        here = cols(m, LANES)
        dn = gate0 * pd[0:ROWS, here] + gate1 * pd[ROWS : 2 * ROWS, here] + dmix[:, here]
        row = mixed[:, here]
        parts[m, 0:8, :] = jnp.sum((dn * row * inv).reshape(ROWS // 8, 8, LANES), axis=0)
        dn = dn * gain(here)
        pd[0:ROWS, here] = dn
        return sums + dn * row

    sums = lax.fori_loop(0, BLOCKS, norm_back, jnp.zeros((ROWS, LANES), F32))
    pull = inv * inv * inv * (jnp.sum(sums, axis=1, keepdims=True) * (1.0 / D))

    def act_back(m, carry):
        here = cols(m, LANES)
        dm = cot[:, here] + (inv * pd[0:ROWS, here] - mixed[:, here] * pull)
        act = pre[:, here]
        s = sigmoid(act)
        dp = dm * (s * (1.0 + act * (1.0 - s)))
        dmix[:, here] = dm
        pd[ROWS : 2 * ROWS, here] = dp
        halo_s[2, :, here] = dp[0:EDGE].astype(BF16)
        halo_s[3, :, here] = dp[ROWS - EDGE : ROWS].astype(BF16)
        return carry

    lax.fori_loop(0, BLOCKS, act_back, 0)
    halo(1, 0).start()
    halo(1, 1).start()

    rows32 = lax.broadcasted_iota(jnp.int32, (32, 512), 0)
    lanes32 = lax.broadcasted_iota(jnp.int32, (32, 512), 1)
    fold = jnp.where(((lanes32 & 255) >> 3) == rows32, 1.0, 0.0).astype(BF16)

    def to_owner(m):
        r = of_expert(m)
        return pltpu.make_async_remote_copy(
            src_ref=ar_src.at[m],
            dst_ref=ar_in.at[back(r)],
            send_sem=a1s.at[m],
            recv_sem=a1r.at[back(r)],
            device_id=peer(r),
            device_id_type=MESH,
        )

    def kernel_grad(i, carry):
        m = (i + ex) % BLOCKS
        here = cols(m, LANES)
        edge = jnp.zeros((EDGE, LANES), F32)
        mid = spread(jnp.concatenate([edge, pd[ROWS : 2 * ROWS, here], edge], axis=0), bound)
        mid = mid[EDGE : EDGE + MID]
        terms = [None] * TAPS
        for shift in range(8):
            rows = gw[m, shift : shift + MID + 24, :]
            for whole in range(4):
                tap = 8 * whole + shift - 1
                if 0 <= tap < TAPS:
                    product = mid * rows[8 * whole : 8 * whole + MID]
                    terms[tap] = jnp.sum(product.reshape(MID // 8, 8, LANES), axis=0)
        terms.append(parts[m, 0:8, :])
        terms = jnp.concatenate(terms, axis=0)
        first = terms.astype(BF16)
        second = (terms - first.astype(F32)).astype(BF16)
        ar_src[m, 0:32, :] = jnp.dot(
            fold, jnp.concatenate([first, second], axis=0), preferred_element_type=F32
        ).astype(BF16)

        @pl.when(m != ex)
        def _():
            to_owner(m).start()

        return carry

    lax.fori_loop(0, BLOCKS, kernel_grad, 0)
    hear(3)

    halo(1, 1).wait_recv()
    halo(1, 0).wait_recv()

    def frames_back(m, carry):
        here = cols(m, LANES)
        gd[0] = spread(widen(0, pd[ROWS : 2 * ROWS, here], 1, m), bound)
        total = correlate(gd, 0, lambda tap: wconv_ref[TAPS - 1 - tap : TAPS - tap, here])
        dfrv[:, here] = dmix[:, here] + gather_back(total, bound)
        return carry

    lax.fori_loop(0, BLOCKS, frames_back, 0)

    def over_columns(k):
        return pltpu.make_async_remote_copy(
            src_ref=mid_src,
            dst_ref=mid_in.at[16 - k],
            send_sem=a2s.at[k],
            recv_sem=a2r.at[16 - k],
            device_id=column(k),
            device_id_type=MESH,
        )

    def to_all(r):
        return pltpu.make_async_remote_copy(
            src_ref=fin_src,
            dst_ref=fin.at[ex],
            send_sem=a3s.at[r],
            recv_sem=a3r.at[ex],
            device_id=peer(r),
            device_id_type=MESH,
        )

    @pl.when(ex < BLOCKS)
    def _():
        def add(q, total):
            pltpu.make_async_remote_copy(
                src_ref=ar_src.at[0],
                dst_ref=ar_in.at[q],
                send_sem=a1s.at[0],
                recv_sem=a1r.at[q],
                device_id=peer(q),
                device_id_type=MESH,
            ).wait_recv()
            return total + ar_in[q].astype(F32)

        total = lax.fori_loop(1, 16, add, ar_src[ex].astype(F32))
        mid_src[...] = total.astype(BF16)

        def send(k, carry):
            over_columns(k).start()
            return carry

        lax.fori_loop(1, 16, send, 0)

    collect(2, ret_y, got_y, py, None)

    def finish(m, carry):
        here = cols(m, LANES)
        outv[:, here] = mixed[:, here] + (
            gate0 * py[0:ROWS, here] + gate1 * py[ROWS : 2 * ROWS, here]
        )
        return carry

    lax.fori_loop(0, BLOCKS, finish, 0)

    @pl.when(ex < BLOCKS)
    def _():
        def add(k, total):
            over_columns(16 - k).wait_recv()
            return total + mid_in[k].astype(F32)

        total = lax.fori_loop(1, 16, add, mid_src[...].astype(F32))
        fin_src[...] = total.astype(BF16)

        def send(r, carry):
            to_all(r).start()
            return carry

        lax.fori_loop(1, 16, send, 0)
        fin[ex] = fin_src[...]

    def spread_out(m, carry):
        @pl.when(m != ex)
        def _():
            pltpu.make_async_remote_copy(
                src_ref=fin_src,
                dst_ref=fin.at[m],
                send_sem=a3s.at[0],
                recv_sem=a3r.at[m],
                device_id=peer(of_expert(m)),
                device_id_type=MESH,
            ).wait_recv()

        here = cols(m, LANES)
        block = fin[m].astype(F32)
        convv[:, here] = block[0:TAPS]
        gainv[here] = block[TAPS]
        routerv[:, here] = block[32:48]
        return carry

    lax.fori_loop(0, BLOCKS, spread_out, 0)

    def sent(r, carry):
        trade(0, send_c, recv_c, r).wait_send()
        trade(1, send_x, recv_x, r).wait_send()
        trade(2, ret_y, got_y, r).wait_send()
        trade(3, ret_d, got_d, r).wait_send()
        return carry

    lax.fori_loop(1, 16, sent, 0)

    def sent_owner(m, carry):
        @pl.when(m != ex)
        def _():
            to_owner(m).wait_send()

        return carry

    lax.fori_loop(0, BLOCKS, sent_owner, 0)

    @pl.when(ex < BLOCKS)
    def _():
        def done(k, carry):
            over_columns(k).wait_send()
            to_all(k).wait_send()
            return carry

        lax.fori_loop(1, 16, done, 0)

    for stage in range(2):
        for side in range(2):
            halo(stage, side).wait_send()


def hand_over(*refs):
    count = (len(refs) - 1) // 2
    copies = [
        pltpu.make_async_copy(refs[n], refs[count + n], refs[-1].at[n]) for n in range(count)
    ]
    for copy in copies:
        copy.start()
    for copy in copies:
        copy.wait()


def on_device(frames, lengths, expert_ids, w_conv, g_norm, w_router, w_up, w_down, cotangent):
    anywhere = pl.BlockSpec(memory_space=pl.ANY)
    wide_f = pltpu.VMEM((ROWS, D), F32)
    half = pltpu.VMEM((ROWS, D), BF16)
    slots = pltpu.VMEM((SLOTS, D), BF16)
    returned = pltpu.VMEM((SLOTS, DE), BF16)
    weight = pltpu.VMEM((D, D), BF16)
    dma = pltpu.SemaphoreType.DMA
    results = (
        jax.ShapeDtypeStruct((ROWS, D), F32),
        jax.ShapeDtypeStruct((ROWS, D), F32),
        jax.ShapeDtypeStruct((TAPS, D), F32),
        jax.ShapeDtypeStruct((D,), F32),
        jax.ShapeDtypeStruct((EXPERTS, D), F32),
    )
    vmem = pl.BlockSpec(memory_space=pltpu.VMEM)
    held = pl.pallas_call(
        body,
        out_shape=tuple(pltpu.VMEM(r.shape, r.dtype) for r in results),
        in_specs=[anywhere] * 9,
        out_specs=(vmem,) * 5,
        scratch_shapes=[
            pltpu.SMEM((2,), jnp.int32), pltpu.VMEM((2, ROWS), jnp.int32),
            pltpu.VMEM((TAPS, D), F32), pltpu.VMEM((D,), F32), pltpu.VMEM((EXPERTS, D), F32),
            half,
            wide_f, wide_f, weight, weight,
            pltpu.VMEM((BLOCKS, SPREAD, LANES), F32),
            pltpu.VMEM((1, SPREAD, LANES), F32),
            wide_f, wide_f, wide_f,
            half, half,
            pltpu.VMEM((SLOTS, ROWS), BF16), pltpu.VMEM((2 * ROWS, SLOTS), BF16),
            slots, slots, slots, slots, slots, slots, returned, returned,
            slots, slots, half,
            pltpu.VMEM((2 * ROWS, D), F32), pltpu.VMEM((2 * ROWS, D), F32),
            pltpu.VMEM((2 * ROWS, LANES), F32),
            pltpu.VMEM((BLOCKS, 8, LANES), F32),
            pltpu.VMEM((4, EDGE, D), BF16), pltpu.VMEM((4, EDGE, D), BF16),
            pltpu.VMEM((BLOCKS, GRADS, LANES), BF16), pltpu.VMEM((16, GRADS, LANES), BF16),
            pltpu.VMEM((GRADS, LANES), BF16), pltpu.VMEM((16, GRADS, LANES), BF16),
            pltpu.VMEM((GRADS, LANES), BF16), pltpu.VMEM((BLOCKS, GRADS, LANES), BF16),
            dma((9,)), dma((4, 16)), dma((4, 16)), dma((4,)), dma((4,)),
            dma((BLOCKS,)), dma((16,)), dma((16,)), dma((16,)), dma((16,)), dma((BLOCKS,)),
            pltpu.SemaphoreType.REGULAR((8,)),
        ],
        compiler_params=pltpu.CompilerParams(
            collective_id=0, has_side_effects=True, vmem_limit_bytes=56 * 2**20
        ),
    )(
        lengths, expert_ids.T, w_conv, g_norm, w_router.T, frames, cotangent, w_up, w_down
    )
    block_out, frames_grad, conv, gain, router = pl.pallas_call(
        hand_over,
        out_shape=results,
        in_specs=[vmem] * 5,
        out_specs=(anywhere,) * 5,
        scratch_shapes=[dma((5,))],
    )(*held)
    return block_out, frames_grad, conv, gain, router.T


def solution(mesh):
    placed = (
        P(("tm", "expert"), None),
        P(),
        P(("tm", "expert"), None),
        P(),
        P(),
        P(),
        P("expert", None, None),
        P("expert", None, None),
        P(("tm", "expert"), None),
    )
    return jax.shard_map(
        on_device,
        mesh=mesh,
        in_specs=placed,
        out_specs=(P(("tm", "expert"), None), P(("tm", "expert"), None), P(), P(), P()),
        check_vma=False,
    )
```

```python
import jax
import jax.numpy as jnp
from jax import lax
from jax.experimental import pallas as pl
from jax.experimental.pallas import tpu as pltpu
from jax.sharding import PartitionSpec as P

EPS = 1e-06
MESH = pl.DeviceIdType.MESH
F32, BF16 = jnp.float32, jnp.bfloat16
EXACT = lax.Precision.HIGHEST

ROWS = 128
D = 1536
TAPS = 31
EDGE = 16
WIDE = ROWS + 2 * EDGE
SPREAD = WIDE + EDGE
MID = ROWS + EDGE
EXPERTS = 16
CAP = 32
SLOTS = EXPERTS * CAP
LANES = 128
BLOCKS = D // LANES
TILE = 256
TILES = D // TILE
GRADS = 48
DE = D + LANES

Y_A, Y_B, Y_C, Y_D = (0, 1), (2, 3), (), ()
EARLY = (0, 1)
NT = (((1,), (1,)), ((), ()))


def sigmoid(v):
    return 0.5 * jnp.tanh(0.5 * v) + 0.5


def spread(wide, bound):
    zeros = jnp.zeros((EDGE, LANES), F32)
    before = jnp.concatenate([wide, zeros], axis=0)
    after = jnp.concatenate([zeros, wide], axis=0)
    row = lax.broadcasted_iota(jnp.int32, (SPREAD, LANES), 0)
    return jnp.where(row < bound, before, jnp.where(row >= bound + EDGE, after, 0.0))


def gather_back(mid, bound):
    row = lax.broadcasted_iota(jnp.int32, (ROWS, LANES), 0) + EDGE
    return jnp.where(row < bound, mid[:ROWS], mid[EDGE:])


def correlate(ref, block, weight_row):
    total = None
    for shift in range(8):
        rows = ref[block, shift : shift + MID + 24, :]
        for whole in range(4):
            tap = 8 * whole + shift - 1
            if 0 <= tap < TAPS:
                term = weight_row(tap) * rows[8 * whole : 8 * whole + MID]
                total = term if total is None else total + term
    return total


def body(
    len_hbm, ids_hbm, wconv_hbm, gain_hbm, wr_hbm, frames_hbm, cot_hbm, wup_hbm, wdn_hbm,
    outv, dfrv, convv, gainv, routerv,
    len_ref, ids_ref, wconv_ref, gain_ref, wr_ref, wrb,
    fr, cot, wup, wdn, gw, gd, pre, mixed, dmix,
    normed, cotb,
    onehot, pick, send_c, recv_c, send_x, recv_x, ret_y, got_y, ret_d, got_d,
    dhid, hid, dup, py, pd, pg, parts,
    halo_s, halo_r, ar_src, ar_in, mid_src, mid_in, fin_src, fin,
    lsem, ssem, rsem, hs, hr, a1s, a1r, a2s, a2r, a3s, a3r, known,
):
    tm, ex = lax.axis_index("tm"), lax.axis_index("expert")
    xl, z = tm // 8, tm % 8
    y, xh, core = ex // 4, (ex // 2) % 2, ex % 2
    lin = tm * EXPERTS + ex

    def peer(r):
        b, dy = r // 4, r % 4
        fx, dc = (dy + b // 2) % 2, b % 2
        return {
            "tm": ((xl + fx) % 2) * 8 + z,
            "expert": ((y + dy) % 4) * 4 + ((xh + fx) % 2) * 2 + (core + dc) % 2,
        }

    def back(r):
        return (r // 4) * 4 + (4 - r % 4) % 4

    def of_expert(e):
        dy, fx, dc = (e // 4 + 4 - y) % 4, (e // 2 + xh) % 2, (e + core) % 2
        return 4 * (2 * ((dy + fx) % 2) + dc) + dy

    def column(k):
        return {"tm": (tm + k) % 16, "expert": ex}

    def along(step):
        return {"tm": xl * 8 + (z + 8 + step) % 8, "expert": ex}

    def beside(step):
        other = (lin + 256 + step) % 256
        return {"tm": other // EXPERTS, "expert": other % EXPERTS}

    barrier = pltpu.get_barrier_semaphore()
    hails = [peer(r) for r in (6, 2, 14, 10, 7, 5, 3, 1, 15, 13, 11, 9, 12, 8, 4)]
    hails = hails[:4] + [beside(1), beside(-1)] + hails[4:] + [along(1), along(-1), column(8)]
    loads = [
        pltpu.make_async_copy(frames_hbm, fr, lsem.at[0]),
        pltpu.make_async_copy(cot_hbm, cot, lsem.at[1]),
        pltpu.make_async_copy(wdn_hbm.at[0], wdn, lsem.at[2]),
        pltpu.make_async_copy(wup_hbm.at[0], wup, lsem.at[3]),
        pltpu.make_async_copy(ids_hbm, ids_ref, lsem.at[4]),
        pltpu.make_async_copy(wconv_hbm, wconv_ref, lsem.at[5]),
        pltpu.make_async_copy(gain_hbm, gain_ref, lsem.at[6]),
        pltpu.make_async_copy(wr_hbm, wr_ref, lsem.at[7]),
        pltpu.make_async_copy(len_hbm, len_ref, lsem.at[8]),
    ]
    for n in (4, 0, 1):
        loads[n].start()
    for other in hails:
        pl.semaphore_signal(barrier, inc=1, device_id=other, device_id_type=MESH)
    for n in (8, 5, 6, 7, 2, 3):
        loads[n].start()

    loads[4].wait()
    def upright(row):
        return jnp.broadcast_to(row.astype(F32), (LANES, ROWS)).T.astype(jnp.int32)

    ids0, ids1 = upright(ids_ref[0:1, :]), upright(ids_ref[1:2, :])

    def relative(e):
        dy, fx, dc = ((e >> 2) - y) & 3, ((e >> 1) & 1) ^ xh, (e & 1) ^ core
        return (((dy ^ fx) & 1) << 3) | (dc << 2) | dy

    rel0, rel1 = relative(ids0), relative(ids1)
    lane = lax.broadcasted_iota(jnp.int32, (ROWS, LANES), 1)
    sub = lax.broadcasted_iota(jnp.int32, (ROWS, LANES), 0)
    names0 = jnp.where(rel0 == lane, 1.0, 0.0).astype(F32)
    names1 = jnp.where(rel1 == lane, 1.0, 0.0).astype(F32)
    names = names0 + names1
    earlier = jnp.where(lane < sub, 1.0, 0.0).astype(F32)
    later = jnp.where(sub < lane, 1.0, 0.0).astype(F32)
    rank = jnp.dot(earlier.astype(BF16), names.astype(BF16), preferred_element_type=F32)
    rank0 = jnp.sum(names0 * rank, axis=1, keepdims=True).astype(jnp.int32)
    rank1 = jnp.sum(names1 * rank, axis=1, keepdims=True).astype(jnp.int32)
    slot0, slot1 = rel0 * CAP + rank0, rel1 * CAP + rank1
    for b in range(4):
        here = slice(b * LANES, (b + 1) * LANES)
        pick[0:ROWS, here] = jnp.where(lane + b * LANES == slot0, 1.0, 0.0).astype(BF16)
        pick[ROWS : 2 * ROWS, here] = jnp.where(lane + b * LANES == slot1, 1.0, 0.0).astype(BF16)
    by_expert = names.T
    order = jnp.dot(by_expert.astype(BF16), later.astype(BF16), preferred_element_type=F32)
    order = jnp.where(by_expert > 0.5, order, -1.0)
    place = lax.broadcasted_iota(jnp.int32, (CAP, LANES), 0).astype(F32)
    for r in range(EXPERTS):
        onehot[r * CAP : (r + 1) * CAP, :] = jnp.where(
            order[r : r + 1, :] == place, 1.0, 0.0
        ).astype(BF16)

    loads[0].wait()
    halo_s[0] = fr[0:EDGE, :].astype(BF16)
    halo_s[1] = fr[ROWS - EDGE : ROWS, :].astype(BF16)

    def halo(stage, side):
        n = 2 * stage + side
        return pltpu.make_async_remote_copy(
            src_ref=halo_s.at[n],
            dst_ref=halo_r.at[2 * stage + 1 - side],
            send_sem=hs.at[n],
            recv_sem=hr.at[2 * stage + 1 - side],
            device_id=beside(2 * side - 1),
            device_id_type=MESH,
        )

    def rows_of(ref, r):
        return ref.at[pl.ds(pl.multiple_of(r * CAP, CAP), CAP), :]

    def trade(kind, src, dst, r):
        return pltpu.make_async_remote_copy(
            src_ref=rows_of(src, r),
            dst_ref=rows_of(dst, back(r)),
            send_sem=ssem.at[kind, r],
            recv_sem=rsem.at[kind, back(r)],
            device_id=peer(r),
            device_id_type=MESH,
        )

    def start_batch(kind, src, dst, b):
        def one(i, carry):
            r = 4 * b + i

            @pl.when(r != 0)
            def _():
                trade(kind, src, dst, r).start()

            return carry

        lax.fori_loop(0, 4, one, 0)

    def arrive_batch(kind, src, dst, b):
        def one(i, carry):
            r = 4 * b + i

            @pl.when(r != 0)
            def _():
                trade(kind, src, dst, back(r)).wait_recv()

            return carry

        lax.fori_loop(0, 4, one, 0)

    def cols(n, width=TILE):
        return pl.ds(pl.multiple_of(n * width, width), width)

    def batch(b):
        return pl.ds(pl.multiple_of(b * ROWS, ROWS), ROWS)

    def fill(source, src, b):
        def part(n, inner):
            src[batch(b), cols(n)] = jnp.dot(
                onehot[batch(b), :], source[:, cols(n)], preferred_element_type=F32
            ).astype(BF16)
            return inner

        lax.fori_loop(0, TILES, part, 0)

    loads[1].wait()

    def narrow(n, carry):
        cotb[:, cols(n)] = cot[:, cols(n)].astype(BF16)
        return carry

    lax.fori_loop(0, TILES, narrow, 0)

    def fill_c(b, carry):
        fill(cotb, send_c, b)
        return carry

    lax.fori_loop(0, 4, fill_c, 0)
    pl.semaphore_wait(barrier, len(hails))
    halo(0, 0).start()
    halo(0, 1).start()

    def go_c(b, carry):
        start_batch(0, send_c, recv_c, b)
        return carry

    lax.fori_loop(0, 4, go_c, 0)
    recv_c[0:CAP, :] = send_c[0:CAP, :]

    def tell(n):
        pl.semaphore_signal(known.at[2 * n], inc=1, device_id=along(1), device_id_type=MESH)
        pl.semaphore_signal(known.at[2 * n + 1], inc=1, device_id=along(-1), device_id_type=MESH)

    def hear(n):
        pl.semaphore_wait(known.at[2 * n], 1)
        pl.semaphore_wait(known.at[2 * n + 1], 1)

    tell(0)

    loads[8].wait()
    loads[5].wait()
    bound = len_ref[0] - lin * ROWS + EDGE
    bound = jnp.where((bound >= 1) & (bound < WIDE), bound, 4 * SPREAD)
    halo(0, 1).wait_recv()
    halo(0, 0).wait_recv()

    def widen(n, middle, stage, m):
        low = jnp.where(lin == 0, 0.0, halo_r[2 * stage, :, cols(m, LANES)].astype(F32))
        high = jnp.where(lin == 255, 0.0, halo_r[2 * stage + 1, :, cols(m, LANES)].astype(F32))
        return jnp.concatenate([low, middle, high], axis=0)

    def conv(m, squares):
        here = cols(m, LANES)
        gw[m] = spread(widen(0, fr[:, here], 0, m), bound)
        total = correlate(gw, m, lambda tap: wconv_ref[tap : tap + 1, here])
        act = gather_back(total, bound)
        row = fr[:, here] + act * sigmoid(act)
        pre[:, here] = act
        mixed[:, here] = row
        return squares + row * row

    squares = lax.fori_loop(0, BLOCKS, conv, jnp.zeros((ROWS, LANES), F32))
    inv = lax.rsqrt(jnp.sum(squares, axis=1, keepdims=True) * (1.0 / D) + EPS)

    loads[6].wait()

    def gain(here):
        return gain_ref[here].reshape(1, LANES)

    def norm(m, carry):
        here = cols(m, LANES)
        normed[:, here] = (mixed[:, here] * inv * gain(here)).astype(BF16)
        return carry

    lax.fori_loop(0, BLOCKS, norm, 0)

    def go_x(b, carry):
        fill(normed, send_x, b)
        start_batch(1, send_x, recv_x, b)
        return carry

    lax.fori_loop(0, 4, go_x, 0)
    recv_x[0:CAP, :] = send_x[0:CAP, :]
    hear(0)
    tell(1)

    loads[7].wait()
    router_f = wr_ref[...]
    part0 = router_f.astype(BF16)
    rest = router_f - part0.astype(F32)
    part1 = rest.astype(BF16)
    wrb[0:16, :] = part0
    wrb[16:32, :] = part1
    wrb[32:48, :] = (rest - part1.astype(F32)).astype(BF16)
    wrb[48:64, :] = part0
    wrb[64:128, :] = jnp.zeros((64, D), BF16)
    logits = lax.dot_general(normed[...], wrb[...], NT, preferred_element_type=F32)
    logits = jnp.where(lane < 48, logits, 0.0)
    low = lane & 15
    top0 = jnp.sum(jnp.where(ids0 == low, logits, 0.0), axis=1, keepdims=True)
    top1 = jnp.sum(jnp.where(ids1 == low, logits, 0.0), axis=1, keepdims=True)
    most = jnp.maximum(top0, top1)
    exp0, exp1 = jnp.exp(top0 - most), jnp.exp(top1 - most)
    gate0, gate1 = exp0 / (exp0 + exp1), exp1 / (exp0 + exp1)

    loads[2].wait()

    def hidden_grad(b, carry):
        arrive_batch(0, send_c, recv_c, b)

        def part(n, inner):
            dhid[batch(b), cols(n)] = lax.dot_general(
                recv_c[batch(b), :], wdn[cols(n), :], NT, preferred_element_type=F32
            ).astype(BF16)
            return inner

        lax.fori_loop(0, TILES, part, 0)
        return carry

    lax.fori_loop(0, 4, hidden_grad, 0)
    hear(1)
    tell(2)
    loads[3].wait()

    def expert(b, carry):
        arrive_batch(1, send_x, recv_x, b)

        def up(n, dots):
            u = jnp.dot(recv_x[batch(b), :], wup[:, cols(n)], preferred_element_type=F32)
            s = sigmoid(u)
            h = (u * s).astype(BF16)
            hid[batch(b), cols(n)] = h
            slope = s * (1.0 + u * (1.0 - s))
            dh = dhid[batch(b), cols(n)].astype(F32)
            dup[:, cols(n)] = (dh * slope).astype(BF16)
            dot = dh * h.astype(F32)
            return dots + dot[:, :LANES] + dot[:, LANES:]

        def rows_grad(n, inner):
            ret_d[batch(b), cols(n)] = lax.dot_general(
                dup[...], wup[cols(n), :], NT, preferred_element_type=F32
            ).astype(BF16)
            return inner

        dots = lax.fori_loop(0, TILES, up, jnp.zeros((ROWS, LANES), F32))
        dgate = jnp.sum(dots, axis=1, keepdims=True)
        first = dgate.astype(BF16).astype(F32)
        ret_d[batch(b), D:DE] = jnp.where(
            lane == 0, first, jnp.where(lane == 1, dgate - first, 0.0)
        ).astype(BF16)
        lax.fori_loop(0, TILES, rows_grad, 0)
        start_batch(3, ret_d, got_d, b)
        return carry

    lax.fori_loop(0, 4, expert, 0)
    got_d[0:CAP, :] = ret_d[0:CAP, :]

    def down(b, carry):
        def part(n, inner):
            ret_y[batch(b), cols(n)] = jnp.dot(
                hid[batch(b), :], wdn[:, cols(n)], preferred_element_type=F32
            ).astype(BF16)
            return inner

        lax.fori_loop(0, TILES, part, 0)
        return carry

    lax.fori_loop(0, 4, down, 0)
    got_y[0:CAP, :] = ret_y[0:CAP, :]

    def go_y(batches):
        for b in batches:
            start_batch(2, ret_y, got_y, b)

    go_y(Y_A)
    hear(2)
    tell(3)

    def collect(kind, src, got, total, tail, batches):
        for b in batches:
            arrive_batch(kind, src, got, b)
            chosen = pick[:, b * ROWS : (b + 1) * ROWS]

            def part(n, carry):
                term = jnp.dot(chosen, got[batch(b), cols(n)], preferred_element_type=F32)
                total[:, cols(n)] = term if b == 0 else total[:, cols(n)] + term
                return carry

            lax.fori_loop(0, TILES, part, 0)
            if tail is not None:
                term = jnp.dot(chosen, got[batch(b), D:DE], preferred_element_type=F32)
                tail[...] = term if b == 0 else tail[...] + term

    collect(3, ret_d, got_d, pd, pg, range(4))
    dgates = jnp.sum(pg[...], axis=1, keepdims=True)
    dtop = gate0 * gate1 * (dgates[0:ROWS] - dgates[ROWS : 2 * ROWS])
    first = dtop.astype(BF16).astype(F32)
    second = dtop - first
    amount = jnp.where(lane < 48, first, jnp.where(lane < 64, second, 0.0))
    dlogits = jnp.where(ids0 == low, amount, 0.0) - jnp.where(ids1 == low, amount, 0.0)
    dlogits_t = dlogits.T[32:64, :].astype(BF16)
    dlogits = dlogits.astype(BF16)

    def router(n, carry):
        both = jnp.dot(dlogits_t, normed[:, cols(n)], preferred_element_type=F32)
        both = (both[0:16] + both[16:32]).astype(BF16)
        ar_src[2 * n, 32:48, :] = both[:, :LANES]
        ar_src[2 * n + 1, 32:48, :] = both[:, LANES:]
        dmix[:, cols(n)] = jnp.dot(dlogits, wrb[:, cols(n)], preferred_element_type=F32)
        return carry

    lax.fori_loop(0, TILES, router, 0)

    def norm_back(m, sums):
        here = cols(m, LANES)
        dn = gate0 * pd[0:ROWS, here] + gate1 * pd[ROWS : 2 * ROWS, here] + dmix[:, here]
        row = mixed[:, here]
        parts[m, 0:8, :] = jnp.sum((dn * row * inv).reshape(ROWS // 8, 8, LANES), axis=0)
        dn = dn * gain(here)
        pd[0:ROWS, here] = dn
        return sums + dn * row

    sums = lax.fori_loop(0, BLOCKS, norm_back, jnp.zeros((ROWS, LANES), F32))
    pull = inv * inv * inv * (jnp.sum(sums, axis=1, keepdims=True) * (1.0 / D))

    def act_back(m, carry):
        here = cols(m, LANES)
        dm = cot[:, here] + (inv * pd[0:ROWS, here] - mixed[:, here] * pull)
        act = pre[:, here]
        s = sigmoid(act)
        dp = dm * (s * (1.0 + act * (1.0 - s)))
        dmix[:, here] = dm
        pd[ROWS : 2 * ROWS, here] = dp
        halo_s[2, :, here] = dp[0:EDGE].astype(BF16)
        halo_s[3, :, here] = dp[ROWS - EDGE : ROWS].astype(BF16)
        return carry

    lax.fori_loop(0, BLOCKS, act_back, 0)
    halo(1, 0).start()
    halo(1, 1).start()

    rows32 = lax.broadcasted_iota(jnp.int32, (32, 512), 0)
    lanes32 = lax.broadcasted_iota(jnp.int32, (32, 512), 1)
    fold = jnp.where(((lanes32 & 255) >> 3) == rows32, 1.0, 0.0).astype(BF16)

    def to_owner(m):
        r = of_expert(m)
        return pltpu.make_async_remote_copy(
            src_ref=ar_src.at[m],
            dst_ref=ar_in.at[back(r)],
            send_sem=a1s.at[m],
            recv_sem=a1r.at[back(r)],
            device_id=peer(r),
            device_id_type=MESH,
        )

    def kernel_grad(i, carry):
        m = (i + ex) % BLOCKS
        here = cols(m, LANES)
        edge = jnp.zeros((EDGE, LANES), F32)
        mid = spread(jnp.concatenate([edge, pd[ROWS : 2 * ROWS, here], edge], axis=0), bound)
        mid = mid[EDGE : EDGE + MID]
        terms = [None] * TAPS
        for shift in range(8):
            rows = gw[m, shift : shift + MID + 24, :]
            for whole in range(4):
                tap = 8 * whole + shift - 1
                if 0 <= tap < TAPS:
                    product = mid * rows[8 * whole : 8 * whole + MID]
                    terms[tap] = jnp.sum(product.reshape(MID // 8, 8, LANES), axis=0)
        terms.append(parts[m, 0:8, :])
        terms = jnp.concatenate(terms, axis=0)
        first = terms.astype(BF16)
        second = (terms - first.astype(F32)).astype(BF16)
        ar_src[m, 0:32, :] = jnp.dot(
            fold, jnp.concatenate([first, second], axis=0), preferred_element_type=F32
        ).astype(BF16)

        @pl.when(m != ex)
        def _():
            to_owner(m).start()

        return carry

    lax.fori_loop(0, BLOCKS, kernel_grad, 0)
    go_y(Y_B)
    hear(3)

    halo(1, 1).wait_recv()
    halo(1, 0).wait_recv()

    def frames_back(m, carry):
        here = cols(m, LANES)
        gd[0] = spread(widen(0, pd[ROWS : 2 * ROWS, here], 1, m), bound)
        total = correlate(gd, 0, lambda tap: wconv_ref[TAPS - 1 - tap : TAPS - tap, here])
        dfrv[:, here] = dmix[:, here] + gather_back(total, bound)
        return carry

    lax.fori_loop(0, BLOCKS, frames_back, 0)

    def over_columns(k):
        return pltpu.make_async_remote_copy(
            src_ref=mid_src,
            dst_ref=mid_in.at[16 - k],
            send_sem=a2s.at[k],
            recv_sem=a2r.at[16 - k],
            device_id=column(k),
            device_id_type=MESH,
        )

    def to_all(r):
        return pltpu.make_async_remote_copy(
            src_ref=fin_src,
            dst_ref=fin.at[ex],
            send_sem=a3s.at[r],
            recv_sem=a3r.at[ex],
            device_id=peer(r),
            device_id_type=MESH,
        )

    @pl.when(ex < BLOCKS)
    def _():
        def add(q, total):
            pltpu.make_async_remote_copy(
                src_ref=ar_src.at[0],
                dst_ref=ar_in.at[q],
                send_sem=a1s.at[0],
                recv_sem=a1r.at[q],
                device_id=peer(q),
                device_id_type=MESH,
            ).wait_recv()
            return total + ar_in[q].astype(F32)

        total = lax.fori_loop(1, 16, add, ar_src[ex].astype(F32))
        mid_src[...] = total.astype(BF16)

        def send(k, carry):
            over_columns(k).start()
            return carry

        lax.fori_loop(1, 16, send, 0)

    go_y(Y_C)
    collect(2, ret_y, got_y, py, None, EARLY)

    @pl.when(ex < BLOCKS)
    def _():
        def add(k, total):
            over_columns(16 - k).wait_recv()
            return total + mid_in[k].astype(F32)

        total = lax.fori_loop(1, 16, add, mid_src[...].astype(F32))
        fin_src[...] = total.astype(BF16)

        def send(r, carry):
            to_all(r).start()
            return carry

        lax.fori_loop(1, 16, send, 0)
        fin[ex] = fin_src[...]

    go_y(Y_D)
    collect(2, ret_y, got_y, py, None, range(len(EARLY), 4))

    def finish(m, carry):
        here = cols(m, LANES)
        outv[:, here] = mixed[:, here] + (
            gate0 * py[0:ROWS, here] + gate1 * py[ROWS : 2 * ROWS, here]
        )
        return carry

    lax.fori_loop(0, BLOCKS, finish, 0)

    def spread_out(m, carry):
        @pl.when(m != ex)
        def _():
            pltpu.make_async_remote_copy(
                src_ref=fin_src,
                dst_ref=fin.at[m],
                send_sem=a3s.at[0],
                recv_sem=a3r.at[m],
                device_id=peer(of_expert(m)),
                device_id_type=MESH,
            ).wait_recv()

        here = cols(m, LANES)
        block = fin[m].astype(F32)
        convv[:, here] = block[0:TAPS]
        gainv[here] = block[TAPS]
        routerv[:, here] = block[32:48]
        return carry

    lax.fori_loop(0, BLOCKS, spread_out, 0)

    def sent(r, carry):
        trade(0, send_c, recv_c, r).wait_send()
        trade(1, send_x, recv_x, r).wait_send()
        trade(2, ret_y, got_y, r).wait_send()
        trade(3, ret_d, got_d, r).wait_send()
        return carry

    lax.fori_loop(1, 16, sent, 0)

    def sent_owner(m, carry):
        @pl.when(m != ex)
        def _():
            to_owner(m).wait_send()

        return carry

    lax.fori_loop(0, BLOCKS, sent_owner, 0)

    @pl.when(ex < BLOCKS)
    def _():
        def done(k, carry):
            over_columns(k).wait_send()
            to_all(k).wait_send()
            return carry

        lax.fori_loop(1, 16, done, 0)

    for stage in range(2):
        for side in range(2):
            halo(stage, side).wait_send()


def hand_over(*refs):
    count = (len(refs) - 1) // 2
    copies = [
        pltpu.make_async_copy(refs[n], refs[count + n], refs[-1].at[n]) for n in range(count)
    ]
    for copy in copies:
        copy.start()
    for copy in copies:
        copy.wait()


def on_device(frames, lengths, expert_ids, w_conv, g_norm, w_router, w_up, w_down, cotangent):
    anywhere = pl.BlockSpec(memory_space=pl.ANY)
    wide_f = pltpu.VMEM((ROWS, D), F32)
    half = pltpu.VMEM((ROWS, D), BF16)
    slots = pltpu.VMEM((SLOTS, D), BF16)
    returned = pltpu.VMEM((SLOTS, DE), BF16)
    weight = pltpu.VMEM((D, D), BF16)
    dma = pltpu.SemaphoreType.DMA
    results = (
        jax.ShapeDtypeStruct((ROWS, D), F32),
        jax.ShapeDtypeStruct((ROWS, D), F32),
        jax.ShapeDtypeStruct((TAPS, D), F32),
        jax.ShapeDtypeStruct((D,), F32),
        jax.ShapeDtypeStruct((EXPERTS, D), F32),
    )
    vmem = pl.BlockSpec(memory_space=pltpu.VMEM)
    held = pl.pallas_call(
        body,
        out_shape=tuple(pltpu.VMEM(r.shape, r.dtype) for r in results),
        in_specs=[anywhere] * 9,
        out_specs=(vmem,) * 5,
        scratch_shapes=[
            pltpu.SMEM((2,), jnp.int32), pltpu.VMEM((2, ROWS), jnp.int32),
            pltpu.VMEM((TAPS, D), F32), pltpu.VMEM((D,), F32), pltpu.VMEM((EXPERTS, D), F32),
            half,
            wide_f, wide_f, weight, weight,
            pltpu.VMEM((BLOCKS, SPREAD, LANES), F32),
            pltpu.VMEM((1, SPREAD, LANES), F32),
            wide_f, wide_f, wide_f,
            half, half,
            pltpu.VMEM((SLOTS, ROWS), BF16), pltpu.VMEM((2 * ROWS, SLOTS), BF16),
            slots, slots, slots, slots, slots, slots, returned, returned,
            slots, slots, half,
            pltpu.VMEM((2 * ROWS, D), F32), pltpu.VMEM((2 * ROWS, D), F32),
            pltpu.VMEM((2 * ROWS, LANES), F32),
            pltpu.VMEM((BLOCKS, 8, LANES), F32),
            pltpu.VMEM((4, EDGE, D), BF16), pltpu.VMEM((4, EDGE, D), BF16),
            pltpu.VMEM((BLOCKS, GRADS, LANES), BF16), pltpu.VMEM((16, GRADS, LANES), BF16),
            pltpu.VMEM((GRADS, LANES), BF16), pltpu.VMEM((16, GRADS, LANES), BF16),
            pltpu.VMEM((GRADS, LANES), BF16), pltpu.VMEM((BLOCKS, GRADS, LANES), BF16),
            dma((9,)), dma((4, 16)), dma((4, 16)), dma((4,)), dma((4,)),
            dma((BLOCKS,)), dma((16,)), dma((16,)), dma((16,)), dma((16,)), dma((BLOCKS,)),
            pltpu.SemaphoreType.REGULAR((8,)),
        ],
        compiler_params=pltpu.CompilerParams(
            collective_id=0, has_side_effects=True, vmem_limit_bytes=56 * 2**20
        ),
    )(
        lengths, expert_ids.T, w_conv, g_norm, w_router.T, frames, cotangent, w_up, w_down
    )
    block_out, frames_grad, conv, gain, router = pl.pallas_call(
        hand_over,
        out_shape=results,
        in_specs=[vmem] * 5,
        out_specs=(anywhere,) * 5,
        scratch_shapes=[dma((5,))],
        compiler_params=pltpu.CompilerParams(vmem_limit_bytes=2**20),
    )(*held)
    return block_out, frames_grad, conv, gain, router.T


def solution(mesh):
    placed = (
        P(("tm", "expert"), None),
        P(),
        P(("tm", "expert"), None),
        P(),
        P(),
        P(),
        P("expert", None, None),
        P("expert", None, None),
        P(("tm", "expert"), None),
    )
    return jax.shard_map(
        on_device,
        mesh=mesh,
        in_specs=placed,
        out_specs=(P(("tm", "expert"), None), P(("tm", "expert"), None), P(), P(), P()),
        check_vma=False,
    )
```

```python
import jax
import jax.numpy as jnp
from jax import lax
from jax.experimental import pallas as pl
from jax.experimental.pallas import tpu as pltpu
from jax.sharding import PartitionSpec as P

EPS = 1e-06
MESH = pl.DeviceIdType.MESH
F32, BF16 = jnp.float32, jnp.bfloat16
EXACT = lax.Precision.HIGHEST

ROWS = 128
D = 1536
TAPS = 31
EDGE = 16
WIDE = ROWS + 2 * EDGE
SPREAD = WIDE + EDGE
MID = ROWS + EDGE
EXPERTS = 16
CAP = 32
SLOTS = EXPERTS * CAP
LANES = 128
BLOCKS = D // LANES
TILE = 256
TILES = D // TILE
GRADS = 48
DE = D + LANES

Y_A, Y_B, Y_C, Y_D = (0, 1), (2, 3), (), ()
EARLY = (0, 1)
NT = (((1,), (1,)), ((), ()))


def sigmoid(v):
    return 0.5 * jnp.tanh(0.5 * v) + 0.5


def spread(wide, bound):
    zeros = jnp.zeros((EDGE, LANES), F32)
    before = jnp.concatenate([wide, zeros], axis=0)
    after = jnp.concatenate([zeros, wide], axis=0)
    row = lax.broadcasted_iota(jnp.int32, (SPREAD, LANES), 0)
    return jnp.where(row < bound, before, jnp.where(row >= bound + EDGE, after, 0.0))


def gather_back(mid, bound):
    row = lax.broadcasted_iota(jnp.int32, (ROWS, LANES), 0) + EDGE
    return jnp.where(row < bound, mid[:ROWS], mid[EDGE:])


def correlate(ref, block, weight_row):
    total = None
    for shift in range(8):
        rows = ref[block, shift : shift + MID + 24, :]
        for whole in range(4):
            tap = 8 * whole + shift - 1
            if 0 <= tap < TAPS:
                term = weight_row(tap) * rows[8 * whole : 8 * whole + MID]
                total = term if total is None else total + term
    return total


def body(
    len_hbm, ids_hbm, wconv_hbm, gain_hbm, wr_hbm, frames_hbm, cot_hbm, wup_hbm, wdn_hbm,
    outv, dfrv, convv, gainv, routerv,
    len_ref, ids_ref, wconv_ref, gain_ref, wr_ref, wrb,
    fr, cot, wup, wdn, gw, gd, pre, mixed, dmix,
    normed, cotb,
    onehot, pick, send_c, recv_c, send_x, recv_x, ret_y, got_y, ret_d, got_d,
    dhid, hid, dup, py, pd, pg, parts,
    halo_s, halo_r, ar_src, ar_in, mid_src, mid_in, fin_src, fin,
    lsem, ssem, rsem, hs, hr, a1s, a1r, a2s, a2r, a3s, a3r, known,
):
    tm, ex = lax.axis_index("tm"), lax.axis_index("expert")
    xl, z = tm // 8, tm % 8
    y, xh, core = ex // 4, (ex // 2) % 2, ex % 2
    lin = tm * EXPERTS + ex

    def peer(r):
        b, dy = r // 4, r % 4
        fx, dc = (dy + b // 2) % 2, b % 2
        return {
            "tm": ((xl + fx) % 2) * 8 + z,
            "expert": ((y + dy) % 4) * 4 + ((xh + fx) % 2) * 2 + (core + dc) % 2,
        }

    def back(r):
        return (r // 4) * 4 + (4 - r % 4) % 4

    def of_expert(e):
        dy, fx, dc = (e // 4 + 4 - y) % 4, (e // 2 + xh) % 2, (e + core) % 2
        return 4 * (2 * ((dy + fx) % 2) + dc) + dy

    def column(k):
        return {"tm": (tm + k) % 16, "expert": ex}

    def along(step):
        return {"tm": xl * 8 + (z + 8 + step) % 8, "expert": ex}

    def beside(step):
        other = (lin + 256 + step) % 256
        return {"tm": other // EXPERTS, "expert": other % EXPERTS}

    barrier = pltpu.get_barrier_semaphore()
    hails = [peer(r) for r in (6, 2, 14, 10, 7, 5, 3, 1, 15, 13, 11, 9, 12, 8, 4)]
    hails = hails[:4] + [beside(1), beside(-1)] + hails[4:] + [along(1), along(-1), column(8)]
    loads = [
        pltpu.make_async_copy(frames_hbm, fr, lsem.at[0]),
        pltpu.make_async_copy(cot_hbm, cot, lsem.at[1]),
        pltpu.make_async_copy(wdn_hbm.at[0], wdn, lsem.at[2]),
        pltpu.make_async_copy(wup_hbm.at[0], wup, lsem.at[3]),
        pltpu.make_async_copy(ids_hbm, ids_ref, lsem.at[4]),
        pltpu.make_async_copy(wconv_hbm, wconv_ref, lsem.at[5]),
        pltpu.make_async_copy(gain_hbm, gain_ref, lsem.at[6]),
        pltpu.make_async_copy(wr_hbm, wr_ref, lsem.at[7]),
        pltpu.make_async_copy(len_hbm, len_ref, lsem.at[8]),
    ]
    for n in (4, 0, 1):
        loads[n].start()
    for other in hails:
        pl.semaphore_signal(barrier, inc=1, device_id=other, device_id_type=MESH)
    for n in (8, 5, 6, 7):
        loads[n].start()

    loads[4].wait()
    def upright(row):
        return jnp.broadcast_to(row.astype(F32), (LANES, ROWS)).T.astype(jnp.int32)

    ids0, ids1 = upright(ids_ref[0:1, :]), upright(ids_ref[1:2, :])

    def relative(e):
        dy, fx, dc = ((e >> 2) - y) & 3, ((e >> 1) & 1) ^ xh, (e & 1) ^ core
        return (((dy ^ fx) & 1) << 3) | (dc << 2) | dy

    rel0, rel1 = relative(ids0), relative(ids1)
    lane = lax.broadcasted_iota(jnp.int32, (ROWS, LANES), 1)
    sub = lax.broadcasted_iota(jnp.int32, (ROWS, LANES), 0)
    names0 = jnp.where(rel0 == lane, 1.0, 0.0).astype(F32)
    names1 = jnp.where(rel1 == lane, 1.0, 0.0).astype(F32)
    names = names0 + names1
    earlier = jnp.where(lane < sub, 1.0, 0.0).astype(F32)
    later = jnp.where(sub < lane, 1.0, 0.0).astype(F32)
    rank = jnp.dot(earlier.astype(BF16), names.astype(BF16), preferred_element_type=F32)
    rank0 = jnp.sum(names0 * rank, axis=1, keepdims=True).astype(jnp.int32)
    rank1 = jnp.sum(names1 * rank, axis=1, keepdims=True).astype(jnp.int32)
    slot0, slot1 = rel0 * CAP + rank0, rel1 * CAP + rank1
    for b in range(4):
        here = slice(b * LANES, (b + 1) * LANES)
        pick[0:ROWS, here] = jnp.where(lane + b * LANES == slot0, 1.0, 0.0).astype(BF16)
        pick[ROWS : 2 * ROWS, here] = jnp.where(lane + b * LANES == slot1, 1.0, 0.0).astype(BF16)
    by_expert = names.T
    order = jnp.dot(by_expert.astype(BF16), later.astype(BF16), preferred_element_type=F32)
    order = jnp.where(by_expert > 0.5, order, -1.0)
    place = lax.broadcasted_iota(jnp.int32, (CAP, LANES), 0).astype(F32)
    for r in range(EXPERTS):
        onehot[r * CAP : (r + 1) * CAP, :] = jnp.where(
            order[r : r + 1, :] == place, 1.0, 0.0
        ).astype(BF16)

    loads[0].wait()
    halo_s[0] = fr[0:EDGE, :].astype(BF16)
    halo_s[1] = fr[ROWS - EDGE : ROWS, :].astype(BF16)

    def halo(stage, side):
        n = 2 * stage + side
        return pltpu.make_async_remote_copy(
            src_ref=halo_s.at[n],
            dst_ref=halo_r.at[2 * stage + 1 - side],
            send_sem=hs.at[n],
            recv_sem=hr.at[2 * stage + 1 - side],
            device_id=beside(2 * side - 1),
            device_id_type=MESH,
        )

    def rows_of(ref, r):
        return ref.at[pl.ds(pl.multiple_of(r * CAP, CAP), CAP), :]

    def trade(kind, src, dst, r):
        return pltpu.make_async_remote_copy(
            src_ref=rows_of(src, r),
            dst_ref=rows_of(dst, back(r)),
            send_sem=ssem.at[kind, r],
            recv_sem=rsem.at[kind, back(r)],
            device_id=peer(r),
            device_id_type=MESH,
        )

    def start_batch(kind, src, dst, b):
        def one(i, carry):
            r = 4 * b + i

            @pl.when(r != 0)
            def _():
                trade(kind, src, dst, r).start()

            return carry

        lax.fori_loop(0, 4, one, 0)

    def arrive_batch(kind, src, dst, b):
        def one(i, carry):
            r = 4 * b + i

            @pl.when(r != 0)
            def _():
                trade(kind, src, dst, back(r)).wait_recv()

            return carry

        lax.fori_loop(0, 4, one, 0)

    def cols(n, width=TILE):
        return pl.ds(pl.multiple_of(n * width, width), width)

    def batch(b):
        return pl.ds(pl.multiple_of(b * ROWS, ROWS), ROWS)

    def fill(source, src, b):
        def part(n, inner):
            src[batch(b), cols(n)] = jnp.dot(
                onehot[batch(b), :], source[:, cols(n)], preferred_element_type=F32
            ).astype(BF16)
            return inner

        lax.fori_loop(0, TILES, part, 0)

    loads[1].wait()

    def narrow(n, carry):
        cotb[:, cols(n)] = cot[:, cols(n)].astype(BF16)
        return carry

    lax.fori_loop(0, TILES, narrow, 0)

    def fill_c(b, carry):
        fill(cotb, send_c, b)
        return carry

    lax.fori_loop(0, 4, fill_c, 0)
    pl.semaphore_wait(barrier, len(hails))

    def go_c(b, carry):
        start_batch(0, send_c, recv_c, b)
        return carry

    for r in range(1, 16):
        trade(0, send_c, recv_c, r).start()
    for n in (2, 3):
        loads[n].start()
    halo(0, 0).start()
    halo(0, 1).start()
    recv_c[0:CAP, :] = send_c[0:CAP, :]

    def tell(n):
        pl.semaphore_signal(known.at[2 * n], inc=1, device_id=along(1), device_id_type=MESH)
        pl.semaphore_signal(known.at[2 * n + 1], inc=1, device_id=along(-1), device_id_type=MESH)

    def hear(n):
        pl.semaphore_wait(known.at[2 * n], 1)
        pl.semaphore_wait(known.at[2 * n + 1], 1)

    tell(0)

    loads[8].wait()
    loads[5].wait()
    bound = len_ref[0] - lin * ROWS + EDGE
    bound = jnp.where((bound >= 1) & (bound < WIDE), bound, 4 * SPREAD)
    halo(0, 1).wait_recv()
    halo(0, 0).wait_recv()

    def widen(n, middle, stage, m):
        low = jnp.where(lin == 0, 0.0, halo_r[2 * stage, :, cols(m, LANES)].astype(F32))
        high = jnp.where(lin == 255, 0.0, halo_r[2 * stage + 1, :, cols(m, LANES)].astype(F32))
        return jnp.concatenate([low, middle, high], axis=0)

    def conv(m, squares):
        here = cols(m, LANES)
        gw[m] = spread(widen(0, fr[:, here], 0, m), bound)
        total = correlate(gw, m, lambda tap: wconv_ref[tap : tap + 1, here])
        act = gather_back(total, bound)
        row = fr[:, here] + act * sigmoid(act)
        pre[:, here] = act
        mixed[:, here] = row
        return squares + row * row

    squares = lax.fori_loop(0, BLOCKS, conv, jnp.zeros((ROWS, LANES), F32))
    inv = lax.rsqrt(jnp.sum(squares, axis=1, keepdims=True) * (1.0 / D) + EPS)

    loads[6].wait()

    def gain(here):
        return gain_ref[here].reshape(1, LANES)

    def norm(m, carry):
        here = cols(m, LANES)
        normed[:, here] = (mixed[:, here] * inv * gain(here)).astype(BF16)
        return carry

    lax.fori_loop(0, BLOCKS, norm, 0)

    def go_x(b, carry):
        fill(normed, send_x, b)
        start_batch(1, send_x, recv_x, b)
        return carry

    lax.fori_loop(0, 4, go_x, 0)
    recv_x[0:CAP, :] = send_x[0:CAP, :]
    hear(0)
    tell(1)

    loads[7].wait()
    router_f = wr_ref[...]
    part0 = router_f.astype(BF16)
    rest = router_f - part0.astype(F32)
    part1 = rest.astype(BF16)
    wrb[0:16, :] = part0
    wrb[16:32, :] = part1
    wrb[32:48, :] = (rest - part1.astype(F32)).astype(BF16)
    wrb[48:64, :] = part0
    wrb[64:128, :] = jnp.zeros((64, D), BF16)
    logits = lax.dot_general(normed[...], wrb[...], NT, preferred_element_type=F32)
    logits = jnp.where(lane < 48, logits, 0.0)
    low = lane & 15
    top0 = jnp.sum(jnp.where(ids0 == low, logits, 0.0), axis=1, keepdims=True)
    top1 = jnp.sum(jnp.where(ids1 == low, logits, 0.0), axis=1, keepdims=True)
    most = jnp.maximum(top0, top1)
    exp0, exp1 = jnp.exp(top0 - most), jnp.exp(top1 - most)
    gate0, gate1 = exp0 / (exp0 + exp1), exp1 / (exp0 + exp1)

    loads[2].wait()

    def hidden_grad(b, carry):
        arrive_batch(0, send_c, recv_c, b)

        def part(n, inner):
            dhid[batch(b), cols(n)] = lax.dot_general(
                recv_c[batch(b), :], wdn[cols(n), :], NT, preferred_element_type=F32
            ).astype(BF16)
            return inner

        lax.fori_loop(0, TILES, part, 0)
        return carry

    lax.fori_loop(0, 4, hidden_grad, 0)
    hear(1)
    tell(2)
    loads[3].wait()

    def expert(b, carry):
        arrive_batch(1, send_x, recv_x, b)

        def up(n, dots):
            u = jnp.dot(recv_x[batch(b), :], wup[:, cols(n)], preferred_element_type=F32)
            s = sigmoid(u)
            h = (u * s).astype(BF16)
            hid[batch(b), cols(n)] = h
            slope = s * (1.0 + u * (1.0 - s))
            dh = dhid[batch(b), cols(n)].astype(F32)
            dup[:, cols(n)] = (dh * slope).astype(BF16)
            dot = dh * h.astype(F32)
            return dots + dot[:, :LANES] + dot[:, LANES:]

        def rows_grad(n, inner):
            ret_d[batch(b), cols(n)] = lax.dot_general(
                dup[...], wup[cols(n), :], NT, preferred_element_type=F32
            ).astype(BF16)
            return inner

        dots = lax.fori_loop(0, TILES, up, jnp.zeros((ROWS, LANES), F32))
        dgate = jnp.sum(dots, axis=1, keepdims=True)
        first = dgate.astype(BF16).astype(F32)
        ret_d[batch(b), D:DE] = jnp.where(
            lane == 0, first, jnp.where(lane == 1, dgate - first, 0.0)
        ).astype(BF16)
        lax.fori_loop(0, TILES, rows_grad, 0)
        start_batch(3, ret_d, got_d, b)
        return carry

    lax.fori_loop(0, 4, expert, 0)
    got_d[0:CAP, :] = ret_d[0:CAP, :]

    def down(b, carry):
        def part(n, inner):
            ret_y[batch(b), cols(n)] = jnp.dot(
                hid[batch(b), :], wdn[:, cols(n)], preferred_element_type=F32
            ).astype(BF16)
            return inner

        lax.fori_loop(0, TILES, part, 0)
        return carry

    lax.fori_loop(0, 4, down, 0)
    got_y[0:CAP, :] = ret_y[0:CAP, :]

    def go_y(batches):
        for b in batches:
            start_batch(2, ret_y, got_y, b)

    go_y(Y_A)
    hear(2)
    tell(3)

    def collect(kind, src, got, total, tail, batches):
        for b in batches:
            arrive_batch(kind, src, got, b)
            chosen = pick[:, b * ROWS : (b + 1) * ROWS]

            def part(n, carry):
                term = jnp.dot(chosen, got[batch(b), cols(n)], preferred_element_type=F32)
                total[:, cols(n)] = term if b == 0 else total[:, cols(n)] + term
                return carry

            lax.fori_loop(0, TILES, part, 0)
            if tail is not None:
                term = jnp.dot(chosen, got[batch(b), D:DE], preferred_element_type=F32)
                tail[...] = term if b == 0 else tail[...] + term

    collect(3, ret_d, got_d, pd, pg, range(4))
    dgates = jnp.sum(pg[...], axis=1, keepdims=True)
    dtop = gate0 * gate1 * (dgates[0:ROWS] - dgates[ROWS : 2 * ROWS])
    first = dtop.astype(BF16).astype(F32)
    second = dtop - first
    amount = jnp.where(lane < 48, first, jnp.where(lane < 64, second, 0.0))
    dlogits = jnp.where(ids0 == low, amount, 0.0) - jnp.where(ids1 == low, amount, 0.0)
    dlogits_t = dlogits.T[32:64, :].astype(BF16)
    dlogits = dlogits.astype(BF16)

    def router(n, carry):
        both = jnp.dot(dlogits_t, normed[:, cols(n)], preferred_element_type=F32)
        both = (both[0:16] + both[16:32]).astype(BF16)
        ar_src[2 * n, 32:48, :] = both[:, :LANES]
        ar_src[2 * n + 1, 32:48, :] = both[:, LANES:]
        dmix[:, cols(n)] = jnp.dot(dlogits, wrb[:, cols(n)], preferred_element_type=F32)
        return carry

    lax.fori_loop(0, TILES, router, 0)

    def norm_back(m, sums):
        here = cols(m, LANES)
        dn = gate0 * pd[0:ROWS, here] + gate1 * pd[ROWS : 2 * ROWS, here] + dmix[:, here]
        row = mixed[:, here]
        parts[m, 0:8, :] = jnp.sum((dn * row * inv).reshape(ROWS // 8, 8, LANES), axis=0)
        dn = dn * gain(here)
        pd[0:ROWS, here] = dn
        return sums + dn * row

    sums = lax.fori_loop(0, BLOCKS, norm_back, jnp.zeros((ROWS, LANES), F32))
    pull = inv * inv * inv * (jnp.sum(sums, axis=1, keepdims=True) * (1.0 / D))

    def act_back(m, carry):
        here = cols(m, LANES)
        dm = cot[:, here] + (inv * pd[0:ROWS, here] - mixed[:, here] * pull)
        act = pre[:, here]
        s = sigmoid(act)
        dp = dm * (s * (1.0 + act * (1.0 - s)))
        dmix[:, here] = dm
        pd[ROWS : 2 * ROWS, here] = dp
        halo_s[2, :, here] = dp[0:EDGE].astype(BF16)
        halo_s[3, :, here] = dp[ROWS - EDGE : ROWS].astype(BF16)
        return carry

    lax.fori_loop(0, BLOCKS, act_back, 0)
    halo(1, 0).start()
    halo(1, 1).start()

    rows32 = lax.broadcasted_iota(jnp.int32, (32, 512), 0)
    lanes32 = lax.broadcasted_iota(jnp.int32, (32, 512), 1)
    fold = jnp.where(((lanes32 & 255) >> 3) == rows32, 1.0, 0.0).astype(BF16)

    def to_owner(m):
        r = of_expert(m)
        return pltpu.make_async_remote_copy(
            src_ref=ar_src.at[m],
            dst_ref=ar_in.at[back(r)],
            send_sem=a1s.at[m],
            recv_sem=a1r.at[back(r)],
            device_id=peer(r),
            device_id_type=MESH,
        )

    def kernel_grad(i, carry):
        m = (i + ex) % BLOCKS
        here = cols(m, LANES)
        edge = jnp.zeros((EDGE, LANES), F32)
        mid = spread(jnp.concatenate([edge, pd[ROWS : 2 * ROWS, here], edge], axis=0), bound)
        mid = mid[EDGE : EDGE + MID]
        terms = [None] * TAPS
        for shift in range(8):
            rows = gw[m, shift : shift + MID + 24, :]
            for whole in range(4):
                tap = 8 * whole + shift - 1
                if 0 <= tap < TAPS:
                    product = mid * rows[8 * whole : 8 * whole + MID]
                    terms[tap] = jnp.sum(product.reshape(MID // 8, 8, LANES), axis=0)
        terms.append(parts[m, 0:8, :])
        terms = jnp.concatenate(terms, axis=0)
        first = terms.astype(BF16)
        second = (terms - first.astype(F32)).astype(BF16)
        ar_src[m, 0:32, :] = jnp.dot(
            fold, jnp.concatenate([first, second], axis=0), preferred_element_type=F32
        ).astype(BF16)

        @pl.when(m != ex)
        def _():
            to_owner(m).start()

        return carry

    lax.fori_loop(0, BLOCKS, kernel_grad, 0)
    go_y(Y_B)
    hear(3)

    halo(1, 1).wait_recv()
    halo(1, 0).wait_recv()

    def frames_back(m, carry):
        here = cols(m, LANES)
        gd[0] = spread(widen(0, pd[ROWS : 2 * ROWS, here], 1, m), bound)
        total = correlate(gd, 0, lambda tap: wconv_ref[TAPS - 1 - tap : TAPS - tap, here])
        dfrv[:, here] = dmix[:, here] + gather_back(total, bound)
        return carry

    lax.fori_loop(0, BLOCKS, frames_back, 0)

    def over_columns(k):
        return pltpu.make_async_remote_copy(
            src_ref=mid_src,
            dst_ref=mid_in.at[16 - k],
            send_sem=a2s.at[k],
            recv_sem=a2r.at[16 - k],
            device_id=column(k),
            device_id_type=MESH,
        )

    def to_all(r):
        return pltpu.make_async_remote_copy(
            src_ref=fin_src,
            dst_ref=fin.at[ex],
            send_sem=a3s.at[r],
            recv_sem=a3r.at[ex],
            device_id=peer(r),
            device_id_type=MESH,
        )

    @pl.when(ex < BLOCKS)
    def _():
        def add(q, total):
            pltpu.make_async_remote_copy(
                src_ref=ar_src.at[0],
                dst_ref=ar_in.at[q],
                send_sem=a1s.at[0],
                recv_sem=a1r.at[q],
                device_id=peer(q),
                device_id_type=MESH,
            ).wait_recv()
            return total + ar_in[q].astype(F32)

        total = lax.fori_loop(1, 16, add, ar_src[ex].astype(F32))
        mid_src[...] = total.astype(BF16)

        for k in (4, 12, 3, 11, 5, 13, 2, 10, 6, 14, 1, 7, 9, 15, 8):
            over_columns(k).start()

    go_y(Y_C)
    collect(2, ret_y, got_y, py, None, EARLY)

    @pl.when(ex < BLOCKS)
    def _():
        def add(k, total):
            over_columns(16 - k).wait_recv()
            return total + mid_in[k].astype(F32)

        total = lax.fori_loop(1, 16, add, mid_src[...].astype(F32))
        fin_src[...] = total.astype(BF16)

        for r in (6, 2, 14, 10, 7, 5, 3, 1, 15, 13, 11, 9, 12, 8, 4):
            to_all(r).start()
        fin[ex] = fin_src[...]

    go_y(Y_D)
    collect(2, ret_y, got_y, py, None, range(len(EARLY), 4))

    def finish(m, carry):
        here = cols(m, LANES)
        outv[:, here] = mixed[:, here] + (
            gate0 * py[0:ROWS, here] + gate1 * py[ROWS : 2 * ROWS, here]
        )
        return carry

    lax.fori_loop(0, BLOCKS, finish, 0)

    def spread_out(m, carry):
        @pl.when(m != ex)
        def _():
            pltpu.make_async_remote_copy(
                src_ref=fin_src,
                dst_ref=fin.at[m],
                send_sem=a3s.at[0],
                recv_sem=a3r.at[m],
                device_id=peer(of_expert(m)),
                device_id_type=MESH,
            ).wait_recv()

        here = cols(m, LANES)
        block = fin[m].astype(F32)
        convv[:, here] = block[0:TAPS]
        gainv[here] = block[TAPS]
        routerv[:, here] = block[32:48]
        return carry

    lax.fori_loop(0, BLOCKS, spread_out, 0)

    def sent(r, carry):
        trade(0, send_c, recv_c, r).wait_send()
        trade(1, send_x, recv_x, r).wait_send()
        trade(2, ret_y, got_y, r).wait_send()
        trade(3, ret_d, got_d, r).wait_send()
        return carry

    lax.fori_loop(1, 16, sent, 0)

    def sent_owner(m, carry):
        @pl.when(m != ex)
        def _():
            to_owner(m).wait_send()

        return carry

    lax.fori_loop(0, BLOCKS, sent_owner, 0)

    @pl.when(ex < BLOCKS)
    def _():
        def done(k, carry):
            over_columns(k).wait_send()
            to_all(k).wait_send()
            return carry

        lax.fori_loop(1, 16, done, 0)

    for stage in range(2):
        for side in range(2):
            halo(stage, side).wait_send()


def hand_over(*refs):
    count = (len(refs) - 1) // 2
    copies = [
        pltpu.make_async_copy(refs[n], refs[count + n], refs[-1].at[n]) for n in range(count)
    ]
    for copy in copies:
        copy.start()
    for copy in copies:
        copy.wait()


def on_device(frames, lengths, expert_ids, w_conv, g_norm, w_router, w_up, w_down, cotangent):
    anywhere = pl.BlockSpec(memory_space=pl.ANY)
    wide_f = pltpu.VMEM((ROWS, D), F32)
    half = pltpu.VMEM((ROWS, D), BF16)
    slots = pltpu.VMEM((SLOTS, D), BF16)
    returned = pltpu.VMEM((SLOTS, DE), BF16)
    weight = pltpu.VMEM((D, D), BF16)
    dma = pltpu.SemaphoreType.DMA
    results = (
        jax.ShapeDtypeStruct((ROWS, D), F32),
        jax.ShapeDtypeStruct((ROWS, D), F32),
        jax.ShapeDtypeStruct((TAPS, D), F32),
        jax.ShapeDtypeStruct((D,), F32),
        jax.ShapeDtypeStruct((EXPERTS, D), F32),
    )
    vmem = pl.BlockSpec(memory_space=pltpu.VMEM)
    held = pl.pallas_call(
        body,
        out_shape=tuple(pltpu.VMEM(r.shape, r.dtype) for r in results),
        in_specs=[anywhere] * 9,
        out_specs=(vmem,) * 5,
        scratch_shapes=[
            pltpu.SMEM((2,), jnp.int32), pltpu.VMEM((2, ROWS), jnp.int32),
            pltpu.VMEM((TAPS, D), F32), pltpu.VMEM((D,), F32), pltpu.VMEM((EXPERTS, D), F32),
            half,
            wide_f, wide_f, weight, weight,
            pltpu.VMEM((BLOCKS, SPREAD, LANES), F32),
            pltpu.VMEM((1, SPREAD, LANES), F32),
            wide_f, wide_f, wide_f,
            half, half,
            pltpu.VMEM((SLOTS, ROWS), BF16), pltpu.VMEM((2 * ROWS, SLOTS), BF16),
            slots, slots, slots, slots, slots, slots, returned, returned,
            slots, slots, half,
            pltpu.VMEM((2 * ROWS, D), F32), pltpu.VMEM((2 * ROWS, D), F32),
            pltpu.VMEM((2 * ROWS, LANES), F32),
            pltpu.VMEM((BLOCKS, 8, LANES), F32),
            pltpu.VMEM((4, EDGE, D), BF16), pltpu.VMEM((4, EDGE, D), BF16),
            pltpu.VMEM((BLOCKS, GRADS, LANES), BF16), pltpu.VMEM((16, GRADS, LANES), BF16),
            pltpu.VMEM((GRADS, LANES), BF16), pltpu.VMEM((16, GRADS, LANES), BF16),
            pltpu.VMEM((GRADS, LANES), BF16), pltpu.VMEM((BLOCKS, GRADS, LANES), BF16),
            dma((9,)), dma((4, 16)), dma((4, 16)), dma((4,)), dma((4,)),
            dma((BLOCKS,)), dma((16,)), dma((16,)), dma((16,)), dma((16,)), dma((BLOCKS,)),
            pltpu.SemaphoreType.REGULAR((8,)),
        ],
        compiler_params=pltpu.CompilerParams(
            collective_id=0, has_side_effects=True, vmem_limit_bytes=56 * 2**20
        ),
    )(
        lengths, expert_ids.T, w_conv, g_norm, w_router.T, frames, cotangent, w_up, w_down
    )
    block_out, frames_grad, conv, gain, router = pl.pallas_call(
        hand_over,
        out_shape=results,
        in_specs=[vmem] * 5,
        out_specs=(anywhere,) * 5,
        scratch_shapes=[dma((5,))],
        compiler_params=pltpu.CompilerParams(vmem_limit_bytes=2**20),
    )(*held)
    return block_out, frames_grad, conv, gain, router.T


def solution(mesh):
    placed = (
        P(("tm", "expert"), None),
        P(),
        P(("tm", "expert"), None),
        P(),
        P(),
        P(),
        P("expert", None, None),
        P("expert", None, None),
        P(("tm", "expert"), None),
    )
    return jax.shard_map(
        on_device,
        mesh=mesh,
        in_specs=placed,
        out_specs=(P(("tm", "expert"), None), P(("tm", "expert"), None), P(), P(), P()),
        check_vma=False,
    )
```
